256 devices in a mesh: rows: 128 (over x_lo, y, z, core), cols: 2 (over x_hi).
Axes of the slice: x: 4 (x_hi: 2, x_lo: 2; x = x_hi * 2 + x_lo), y: 4, z: 8, core: 2. Of those that a mesh axis runs over, the one named last changes fastest.
Arguments:
- features: bfloat16 [32768, 128], P('rows', 'cols'), may hold values from -6 to 6
- adj_tiles: bfloat16 [12288, 128, 128], P('rows'), may hold values from -0.109375 to 0.109375
- tile_src: int32 [12288], P('rows'), may hold values from 0 to 255, as said below
- tile_dst: int32 [12288], P('rows'), may hold values from 0 to 1, as said below
- tile_count: int32 [128], P('rows'), may hold values from 24 to 96, as said below
- cluster_size: int32 [256], P('rows'), may hold values from 64 to 128, as said below
- weight: bfloat16 [128, 256], P(None, 'cols'), may hold values from -0.5 to 0.5
- bias: float32 [256], P('cols'), may hold values from -3 to 3
- grad_out: bfloat16 [32768, 256], P('rows', 'cols'), may hold values from -6 to 6
Outputs:
- hidden: bfloat16 [32768, 256], P('rows', 'cols')
- grad_weight: float32 [128, 256], P(None, 'cols')
- grad_bias: float32 [256], P('cols')
- grad_features: bfloat16 [32768, 128], P('rows', 'cols')
The draws below stay inside these ranges and needn't reach their ends.
Inputs may be any that keep to these rules, and one draw needn't show every extreme that they name: In row group r, slots 0 to tile_count[r] - 1 of its 96 slots hold tiles, in non-decreasing order of tile_src; the later slots are unused: their tile_src and tile_dst hold 0, and their adj_tiles hold arbitrary values that must not contribute. A used slot's column cluster belongs to row group r itself or to a row group whose index differs from r in exactly one bit (row group g holds clusters g * 2 to g * 2 + 1). Equal (row, column) pairs may repeat and then add. `tile_dst`: unused slots hold 0. `tile_count`: some row groups use all 96 slots. `cluster_size`: the real nodes of a cluster are its first ones; some cluster is full.
All inputs are finite; a program needn't handle non-finite values.
Results may differ from the reference program's by a relative error of at most 0.006.
Values may be sent and summed in bfloat16 or wider, within the bound.
A program may use at most 64 MiB of HBM per device.

```python
import math
import jax
import jax.numpy as jnp
from jax import lax

F = 128
HID = 256
CLS = 128
TPC = 48
CL_DEV = 2
TILES_DEV = 96
CLUSTERS = 256
NODES = 32768
ROW_SLOTS = 12288
LEVELS = 7


def tile_layout(key):
    group_count = ROW_SLOTS // TILES_DEV
    key_rank, key_light, key_level, key_within, key_dst = jax.random.split(jax.random.fold_in(key, 11), 5)
    row_rank = jax.random.permutation(key_rank, group_count)
    light_count = jax.random.randint(key_light, (group_count,), TILES_DEV // 4, TILES_DEV // 2 + 1)
    live_count = jnp.where(row_rank < max(group_count // 8, 1), TILES_DEV, light_count).astype(jnp.int32)
    slot_ids = jnp.arange(TILES_DEV, dtype=jnp.int32)
    in_use = slot_ids[None, :] < live_count[:, None]
    group_ids = jnp.arange(group_count, dtype=jnp.int32)[:, None]
    level = jax.random.randint(key_level, (group_count, TILES_DEV), 0, LEVELS + 1).astype(jnp.int32)
    flipped = jnp.bitwise_xor(group_ids, jnp.left_shift(jnp.ones_like(level), jnp.minimum(level, LEVELS - 1)))
    neighbour = jnp.where(level == LEVELS, group_ids, flipped)
    within = jax.random.randint(key_within, (group_count, TILES_DEV), 0, CL_DEV).astype(jnp.int32)
    drawn_src = neighbour * CL_DEV + within
    drawn_src = drawn_src.at[0, 0].set(0)
    drawn_src = drawn_src.at[group_count - 1, 0].set(CLUSTERS - 1)
    ordered = jnp.sort(jnp.where(in_use, drawn_src, CLUSTERS), axis=1)
    sources = jnp.where(in_use, ordered, 0).reshape(-1).astype(jnp.int32)
    drawn_dst = jax.random.randint(key_dst, (group_count, TILES_DEV), 0, CL_DEV)
    targets = jnp.where(in_use, drawn_dst, 0).reshape(-1).astype(jnp.int32)
    return (sources, targets, live_count)


def draw_tile_src(key, part):
    return tile_layout(key)[0]


def draw_tile_dst(key, part):
    return tile_layout(key)[1]


def draw_tile_count(key, part):
    return tile_layout(key)[2]


def draw_cluster_size(key, part):
    key_size, key_full = jax.random.split(jax.random.fold_in(key, 23))
    sizes = jax.random.randint(key_size, (CLUSTERS,), CLS // 2, CLS + 1)
    full_at = jax.random.randint(key_full, (), 0, CLUSTERS)
    return jnp.where(jnp.arange(CLUSTERS) == full_at, CLS, sizes).astype(jnp.int32)


def steps_of(key, extent, cuts, low, top_value):
    loudness = 1.0
    for dim, blocks in cuts:
        steps = jax.random.uniform(jax.random.fold_in(jax.random.fold_in(key, 6), dim), (blocks,), jnp.float32, low / len(cuts), top_value / len(cuts))
        loudness = loudness * jnp.repeat(jnp.exp(steps), extent[dim] // blocks).reshape((-1,) + (1,) * (len(extent) - 1 - dim))
    return loudness


def normal_values(stream_key, extent, spread, limit, cuts=(), kind=jnp.bfloat16):
    factor_of = steps_of(stream_key, extent, cuts, -0.22, 0.18) if cuts else 1.0
    drawn = jax.random.normal(stream_key, extent, jnp.float32) * spread * factor_of
    return jnp.minimum(jnp.maximum(drawn, -limit), limit).astype(kind)


def setup_inputs(seed: int = 0) -> dict:
    splits = jax.random.split(jax.random.key(seed), 10)
    features = normal_values(splits[0], (NODES, F), 1.0, 6.0, ((0, 128), (1, 2)))
    adj_tiles = normal_values(splits[1], (ROW_SLOTS, CLS, CLS), (CLS * TPC // 2) ** -0.5, 0.109375, ((0, 128),))
    tile_src = draw_tile_src(jax.random.fold_in(splits[9], 71), 0)
    tile_dst = draw_tile_dst(jax.random.fold_in(splits[9], 71), 0)
    tile_count = draw_tile_count(jax.random.fold_in(splits[9], 71), 0)
    cluster_size = draw_cluster_size(jax.random.fold_in(splits[9], 71), 0)
    weight = normal_values(splits[6], (F, HID), F ** -0.5, 0.5, ((1, 2),))
    bias = normal_values(splits[7], (HID,), 0.5, 3.0, ((0, 2),), jnp.float32)
    grad_out = normal_values(splits[8], (NODES, HID), 1.0, 6.0, ((0, 128), (1, 2)))
    return dict(features=features, adj_tiles=adj_tiles, tile_src=tile_src, tile_dst=tile_dst, tile_count=tile_count, cluster_size=cluster_size, weight=weight, bias=bias, grad_out=grad_out)


def reference(features, adj_tiles, tile_src, tile_dst, tile_count, cluster_size, weight, bias, grad_out):
    row_groups = CLUSTERS // CL_DEV
    node_ids = jnp.arange(CLS, dtype=jnp.int32)
    live_node = (node_ids[None, :] < cluster_size[:, None]).astype(jnp.float32).reshape(NODES, 1)
    masked = (features.astype(jnp.float32) * live_node).astype(jnp.bfloat16)
    blocks = masked.reshape(CLUSTERS, CLS, F)
    tile_data = adj_tiles.reshape(row_groups, TILES_DEV, CLS, CLS)
    sources = tile_src.reshape(row_groups, TILES_DEV)
    targets = tile_dst.reshape(row_groups, TILES_DEV)
    slot_ids = jnp.arange(TILES_DEV, dtype=jnp.int32)

    def forward_row(packed):
        group_tiles, group_src, group_dst, group_count = packed
        in_use = (slot_ids < group_count).astype(jnp.float32)
        taken_rows = blocks[group_src].astype(jnp.float32)
        products = jnp.einsum('tij,tjf->tif', group_tiles.astype(jnp.float32), taken_rows) * in_use[:, None, None]
        return jnp.zeros((CL_DEV, CLS, F), jnp.float32).at[group_dst].add(products)
    agg = lax.map(forward_row, (tile_data, sources, targets, tile_count)).reshape(NODES, F).astype(jnp.bfloat16)
    pre_activation = jnp.dot(agg, weight, preferred_element_type=jnp.float32) + bias
    sigmoid_pre = jax.nn.sigmoid(pre_activation)
    hidden = (pre_activation * sigmoid_pre * live_node).astype(jnp.bfloat16)
    grad_pre = (grad_out.astype(jnp.float32) * sigmoid_pre * (1.0 + pre_activation * (1.0 - sigmoid_pre)) * live_node).astype(jnp.bfloat16)
    grad_scale = 1.0 / math.sqrt(NODES)
    grad_weight = jnp.dot(agg.T, grad_pre, preferred_element_type=jnp.float32) * grad_scale
    grad_bias = lax.optimization_barrier(jnp.sum(grad_pre.astype(jnp.float32), axis=0)) * grad_scale
    grad_agg = jnp.dot(grad_pre, weight.T, preferred_element_type=jnp.float32).astype(jnp.bfloat16).reshape(CLUSTERS, CLS, F)

    def backward_row(totals, packed):
        group_tiles, group_src, group_dst, group_count, group_index = packed
        in_use = (slot_ids < group_count).astype(jnp.float32)
        taken_rows = grad_agg[group_index * CL_DEV + group_dst].astype(jnp.float32)
        products = jnp.einsum('tji,tjf->tif', group_tiles.astype(jnp.float32), taken_rows) * in_use[:, None, None]
        return (totals.at[group_src].add(products), None)
    group_ids = jnp.arange(row_groups, dtype=jnp.int32)
    totals, unused = lax.scan(backward_row, jnp.zeros((CLUSTERS, CLS, F), jnp.float32), (tile_data, sources, targets, tile_count, group_ids))
    grad_features = (totals.reshape(NODES, F) * live_node).astype(jnp.bfloat16)
    return (hidden, grad_weight, grad_bias, grad_features)
```

```python
import functools
import math

import jax
import jax.numpy as jnp
from jax import lax
from jax.experimental import pallas as pl
from jax.experimental.pallas import tpu as pltpu
from jax.sharding import PartitionSpec as P

F32 = jnp.float32
BF16 = jnp.bfloat16
MESH = pl.DeviceIdType.MESH


def flip_bits(index, mask):
    out = index
    bit = 1
    while bit <= mask:
        if mask & bit:
            out = out + bit - 2 * bit * ((index // bit) % 2)
        bit *= 2
    return out


def layer_kernel(
    plan,
    src_ref,
    dst_ref,
    count_ref,
    size_ref,
    feat_hbm,
    tiles_hbm,
    weight_hbm,
    bias_hbm,
    gout_hbm,
    hidden_ref,
    gw_ref,
    gb_ref,
    gf_ref,
    feat,
    tiles,
    weights,
    biases,
    gouts,
    packed,
    sums,
    dense,
    agg_own,
    agg_other,
    stage,
    fold_in,
    fold_mid,
    fold_all,
    give,
    take,
    own_back,
    load_sem,
    x_send,
    x_recv,
    p_send,
    p_recv,
    c_send,
    c_recv,
    r1_send,
    r1_recv,
    r2_send,
    r2_recv,
    r3_send,
    r3_recv,
):
    near, wide, deep, scale = plan
    levels = len(near)
    wide_count, deep_count = len(wide), len(deep)
    me = lax.axis_index("rows")
    col = lax.axis_index("cols")
    slots = tiles.shape[0]
    tall = tiles.shape[1]

    def remote(src, dst, send, recv, mask):
        who = {"cols": 1 - col} if mask is None else {"rows": flip_bits(me, mask)}
        return pltpu.make_async_remote_copy(
            src_ref=src,
            dst_ref=dst,
            send_sem=send,
            recv_sem=recv,
            device_id=who,
            device_id_type=MESH,
        )

    loads = [
        pltpu.make_async_copy(feat_hbm, feat, load_sem.at[0]),
        pltpu.make_async_copy(weight_hbm, weights.at[0], load_sem.at[1]),
        pltpu.make_async_copy(bias_hbm, biases.at[0], load_sem.at[2]),
        pltpu.make_async_copy(gout_hbm, gouts.at[0], load_sem.at[3]),
        pltpu.make_async_copy(tiles_hbm, tiles, load_sem.at[4]),
    ]
    for load in loads:
        load.start()

    peers = sorted(set(near) | set(wide[1:]) | set(deep[1:]))
    barrier = pltpu.get_barrier_semaphore()
    for mask in peers:
        pl.semaphore_signal(
            barrier, inc=1, device_id={"rows": flip_bits(me, mask)}, device_id_type=MESH
        )
    pl.semaphore_signal(barrier, inc=1, device_id={"cols": 1 - col}, device_id_type=MESH)

    lanes = lax.broadcasted_iota(jnp.int32, (tall, 2 * feat.shape[1]), 1)
    left = lanes < feat.shape[1]
    node = lax.broadcasted_iota(jnp.int32, (tall, tall), 0)
    live = [(node < size_ref[c]).astype(F32) for c in range(2)]
    half = feat.shape[1]

    loads[0].wait()
    pair = jnp.concatenate([feat[:tall, :], feat[tall:, :]], axis=1).astype(F32)
    packed[levels] = jnp.where(left, pair * live[0], pair * live[1]).astype(BF16)

    pl.semaphore_wait(barrier, len(peers) + 1)

    feature_copies = [
        remote(packed.at[levels], packed.at[k], x_send.at[k], x_recv.at[k], near[k])
        for k in range(levels)
    ]
    for copy in feature_copies[::-1]:
        copy.start()
    side_copies = [
        remote(weight_hbm, weights.at[1], p_send.at[0], p_recv.at[0], None),
        remote(bias_hbm, biases.at[1], p_send.at[1], p_recv.at[1], None),
        remote(gout_hbm, gouts.at[1], p_send.at[2], p_recv.at[2], None),
    ]
    for copy in side_copies:
        copy.start()

    clusters = []
    for k in range(levels + 1):
        group = flip_bits(me, near[k]) if k < levels else me
        clusters += [group * 2, group * 2 + 1]
    count = count_ref[0]
    for load in loads[1:]:
        load.wait()

    def one_tile(t, carried):
        first, second, prev, lasts = carried
        src = src_ref[t]
        used = t < count
        keep = (src == prev) & used
        to_second = dst_ref[t] == 1
        tile = tiles[t].astype(F32)
        zero = jnp.zeros_like(tile)
        first = jnp.where(keep, first, zero) + jnp.where(used & (~to_second), tile, zero)
        second = jnp.where(keep, second, zero) + jnp.where(used & to_second, tile, zero)
        sums[0, t] = first.astype(BF16)
        sums[1, t] = second.astype(BF16)
        lasts = tuple(
            jnp.where(used & (src == cluster), t, last)
            for last, cluster in zip(lasts, clusters)
        )
        return first, second, src, lasts

    blank = jnp.zeros((tall, tall), F32)
    lasts = lax.fori_loop(
        0,
        slots,
        one_tile,
        (blank, blank, jnp.int32(-1), tuple(jnp.int32(-1) for _ in clusters)),
    )[3]
    for j, last in enumerate(lasts):
        at = jnp.maximum(last, 0)
        for d in range(2):
            block = sums[d, at]
            dense[j // 2, d * tall : (d + 1) * tall, (j % 2) * tall : (j % 2 + 1) * tall] = (
                jnp.where(last >= 0, block, jnp.zeros_like(block))
            )

    total = None
    for k in [levels] + list(range(levels)):
        if k < levels:
            feature_copies[k].wait_recv()
        block = packed[k]
        none = jnp.zeros_like(block)
        rows = jnp.concatenate(
            [jnp.where(left, block, none), jnp.where(left, none, block)], axis=0
        )
        term = jnp.dot(dense[k], rows, preferred_element_type=F32)
        total = term if total is None else total + term
    total = total + pltpu.roll(total, half, 1)
    agg_own[...] = jnp.where(left, total[:tall], total[tall:]).astype(BF16)
    agg_copy = remote(agg_own, agg_other, p_send.at[3], p_recv.at[3], None)
    agg_copy.start()
    for copy in side_copies:
        copy.wait_recv()
    agg_copy.wait_recv()

    mine, other = agg_own[...].astype(F32), agg_other[...].astype(F32)
    low = jnp.where(col == 0, mine, other)
    high = jnp.where(col == 0, other, mine)
    agg = jnp.concatenate(
        [
            jnp.where(left, low, pltpu.roll(high, half, 1)),
            jnp.where(left, pltpu.roll(low, half, 1), high),
        ],
        axis=0,
    ).astype(BF16)
    live_all = jnp.concatenate(live, axis=0)
    grads = []
    for side in range(2):
        pre = jnp.dot(agg, weights[side], preferred_element_type=F32) + biases[side]
        gate = jax.nn.sigmoid(pre)
        if side == 0:
            hidden_ref[...] = (pre * gate * live_all).astype(BF16)
        grads.append(
            (
                gouts[side].astype(F32) * gate * (1.0 + pre * (1.0 - gate)) * live_all
            ).astype(BF16)
        )

    by_rows = (((0,), (0,)), ((), ()))
    grad_weight = lax.dot_general(agg, grads[0], by_rows, preferred_element_type=F32)
    chunk = grad_weight.shape[0] // wide_count
    grad_bias = jnp.sum(grads[0].astype(F32), axis=0, keepdims=True)
    stage[:, :chunk, :] = grad_weight.reshape(wide_count, chunk, grad_weight.shape[1])
    stage[:, chunk:, :] = jnp.broadcast_to(
        grad_bias[None], (wide_count, stage.shape[1] - chunk, grad_weight.shape[1])
    )

    def place(index, masks):
        out, bit = 0, 1
        while bit < len(masks):
            out = out + bit * ((index // masks[bit]) % 2)
            bit *= 2
        return out

    my_wide, my_deep = place(me, wide), place(me, deep)
    scatter_copies = [
        remote(
            stage.at[place(flip_bits(me, wide[m]), wide)],
            fold_in.at[my_wide],
            r1_send.at[m],
            r1_recv.at[m],
            wide[m],
        )
        for m in range(1, wide_count)
    ]
    for copy in scatter_copies:
        copy.start()
    fold_in[my_wide] = stage[my_wide]

    own_rows = pl.ds(pl.multiple_of(col * half, half), half)
    by_lanes = (((1,), (1,)), ((), ()))
    grad_agg = sum(
        lax.dot_general(
            weights[side, own_rows, :], grads[side], by_lanes, preferred_element_type=F32
        )
        for side in range(2)
    ).astype(BF16)
    back_copies = [
        remote(give.at[k], take.at[k], c_send.at[k], c_recv.at[k], near[k])
        for k in range(levels)
    ]
    for k in range(levels - 1, -1, -1):
        give[k] = jnp.dot(grad_agg, dense[k], preferred_element_type=F32).astype(BF16)
        back_copies[k].start()
    own_back[...] = jnp.dot(grad_agg, dense[levels], preferred_element_type=F32)

    for m in range(1, wide_count):
        remote(
            stage.at[0],
            fold_in.at[place(flip_bits(me, wide[m]), wide)],
            r1_send.at[m],
            r1_recv.at[m],
            wide[m],
        ).wait_recv()
    part = fold_in[0]
    for m in range(1, wide_count):
        part = part + fold_in[m]
    fold_mid[my_deep] = part
    deep_copies = [
        remote(
            fold_mid.at[my_deep], fold_mid.at[my_deep], r2_send.at[m], r2_recv.at[m], deep[m]
        )
        for m in range(1, deep_count)
    ]
    for copy in deep_copies:
        copy.start()

    back = own_back[...]
    for k in range(levels):
        back_copies[k].wait_recv()
        back = back + take[k].astype(F32)
    node_lane = lax.broadcasted_iota(jnp.int32, (half, tall), 1)
    for c in range(2):
        piece = back[:, c * tall : (c + 1) * tall]
        piece = jnp.where(node_lane < size_ref[c], piece, jnp.zeros_like(piece))
        gf_ref[c * tall : (c + 1) * tall, :] = piece.T.astype(BF16)

    for m in range(1, deep_count):
        remote(
            fold_mid.at[my_deep],
            fold_mid.at[place(flip_bits(me, deep[m]), deep)],
            r2_send.at[m],
            r2_recv.at[m],
            deep[m],
        ).wait_recv()
    part = fold_mid[0]
    for m in range(1, deep_count):
        part = part + fold_mid[m]
    part = part * scale
    gb_ref[...] = part[chunk : chunk + 1, :]
    fold_all[my_wide] = part[:chunk]
    gather_copies = [
        remote(
            fold_all.at[my_wide], fold_all.at[my_wide], r3_send.at[m], r3_recv.at[m], wide[m]
        )
        for m in range(1, wide_count)
    ]
    for copy in gather_copies:
        copy.start()
    for m in range(1, wide_count):
        remote(
            fold_all.at[my_wide],
            fold_all.at[place(flip_bits(me, wide[m]), wide)],
            r3_send.at[m],
            r3_recv.at[m],
            wide[m],
        ).wait_recv()
    gw_ref[...] = fold_all[...].reshape(gw_ref.shape)

    for copy in (
        feature_copies
        + side_copies
        + [agg_copy]
        + scatter_copies
        + back_copies
        + deep_copies
        + gather_copies
    ):
        copy.wait_send()


def group_masks(bits):
    return [
        sum(1 << bit for place, bit in enumerate(bits) if m >> place & 1)
        for m in range(1 << len(bits))
    ]


def solution(mesh):
    row_groups = mesh.shape["rows"]
    levels = row_groups.bit_length() - 1
    deep_bits = [bit for bit in range(levels) if 1 <= bit <= (3 if levels > 4 else 1)]
    wide_bits = [bit for bit in range(levels) if bit not in deep_bits]
    near = [1 << bit for bit in range(levels)]
    wide, deep = group_masks(wide_bits), group_masks(deep_bits)

    def local(
        features, adj_tiles, tile_src, tile_dst, tile_count, cluster_size, weight, bias, grad_out
    ):
        slots, tall, _ = adj_tiles.shape
        nodes, half = features.shape
        wide_feat, units = weight.shape
        chunk = wide_feat // len(wide)
        dma = pltpu.SemaphoreType.DMA
        plan = (near, wide, deep, 1.0 / math.sqrt(nodes * row_groups))
        smem = pl.BlockSpec(memory_space=pltpu.SMEM)
        vmem = pl.BlockSpec(memory_space=pltpu.VMEM)
        hbm = pl.BlockSpec(memory_space=pltpu.HBM)
        hidden, grad_weight, grad_bias, grad_features = pl.pallas_call(
            functools.partial(layer_kernel, plan),
            out_shape=(
                jax.ShapeDtypeStruct((nodes, units), BF16),
                jax.ShapeDtypeStruct((wide_feat, units), F32),
                jax.ShapeDtypeStruct((1, units), F32),
                jax.ShapeDtypeStruct((nodes, half), BF16),
            ),
            in_specs=[smem] * 4 + [hbm] * 5,
            out_specs=(vmem,) * 4,
            scratch_shapes=[
                pltpu.VMEM((nodes, half), BF16),
                pltpu.VMEM((slots, tall, tall), BF16),
                pltpu.VMEM((2, wide_feat, units), BF16),
                pltpu.VMEM((2, 1, units), F32),
                pltpu.VMEM((2, nodes, units), BF16),
                pltpu.VMEM((levels + 1, tall, 2 * half), BF16),
                pltpu.VMEM((2, slots, tall, tall), BF16),
                pltpu.VMEM((levels + 1, nodes, nodes), BF16),
                pltpu.VMEM((tall, 2 * half), BF16),
                pltpu.VMEM((tall, 2 * half), BF16),
                pltpu.VMEM((len(wide), chunk + 8, units), F32),
                pltpu.VMEM((len(wide), chunk + 8, units), F32),
                pltpu.VMEM((len(deep), chunk + 8, units), F32),
                pltpu.VMEM((len(wide), chunk, units), F32),
                pltpu.VMEM((levels, half, nodes), BF16),
                pltpu.VMEM((levels, half, nodes), BF16),
                pltpu.VMEM((half, nodes), F32),
                dma((5,)),
                dma((levels,)),
                dma((levels,)),
                dma((4,)),
                dma((4,)),
                dma((levels,)),
                dma((levels,)),
                dma((len(wide),)),
                dma((len(wide),)),
                dma((len(deep),)),
                dma((len(deep),)),
                dma((len(wide),)),
                dma((len(wide),)),
            ],
            compiler_params=pltpu.CompilerParams(
                collective_id=0, has_side_effects=True, vmem_limit_bytes=40 * 1024 * 1024
            ),
            name="graph_layer",
        )(
            tile_src,
            tile_dst,
            tile_count,
            cluster_size,
            features,
            adj_tiles,
            weight,
            bias.reshape(1, units),
            grad_out,
        )
        return hidden, grad_weight, grad_bias.reshape(units), grad_features

    return jax.shard_map(
        local,
        mesh=mesh,
        in_specs=(
            P("rows", "cols"),
            P("rows", None, None),
            P("rows"),
            P("rows"),
            P("rows"),
            P("rows"),
            P(None, "cols"),
            P("cols"),
            P("rows", "cols"),
        ),
        out_specs=(P("rows", "cols"), P(None, "cols"), P("cols"), P("rows", "cols")),
        check_vma=False,
    )
```

```python
import functools
import math

import jax
import jax.numpy as jnp
from jax import lax
from jax.experimental import pallas as pl
from jax.experimental.pallas import tpu as pltpu
from jax.sharding import PartitionSpec as P

F32 = jnp.float32
BF16 = jnp.bfloat16
MESH = pl.DeviceIdType.MESH
EARLY = 1


def flip_bits(index, mask):
    out = index
    bit = 1
    while bit <= mask:
        if mask & bit:
            out = out + bit - 2 * bit * ((index // bit) % 2)
        bit *= 2
    return out


def place(index, masks):
    out, bit = 0, 1
    while bit < len(masks):
        out = out + bit * ((index // masks[bit]) % 2)
        bit *= 2
    return out


def layer_kernel(
    plan,
    src_hbm,
    dst_hbm,
    count_ref,
    size_hbm,
    feat_hbm,
    tiles_hbm,
    weight_hbm,
    bias_hbm,
    gout_hbm,
    hidden_ref,
    gw_ref,
    gb_ref,
    gf_ref,
    src_ref,
    dst_ref,
    size_ref,
    feat,
    tiles,
    weights,
    biases,
    gouts,
    packed,
    sums,
    dense,
    agg,
    turned,
    gout_turned,
    bias_turned,
    stage,
    fold_in,
    fold_mid,
    fold_all,
    give,
    take,
    own_back,
    load_sem,
    tile_sem,
    x_send,
    x_recv,
    p_send,
    p_recv,
    c_send,
    c_recv,
    r1_send,
    r1_recv,
    r2_send,
    r2_recv,
    r3_send,
    r3_recv,
):
    near, wide, deep, scale, early = plan
    levels = len(near)
    wide_count, deep_count = len(wide), len(deep)
    me = lax.axis_index("rows")
    col = lax.axis_index("cols")
    slots, tall, _ = tiles.shape
    half, nodes = feat.shape
    parts = tile_sem.shape[0]
    part_slots = slots // parts

    def remote(src, dst, send, recv, mask):
        who = {"cols": 1 - col} if mask is None else {"rows": flip_bits(me, mask)}
        return pltpu.make_async_remote_copy(
            src_ref=src,
            dst_ref=dst,
            send_sem=send,
            recv_sem=recv,
            device_id=who,
            device_id_type=MESH,
        )

    peers = sorted(set(near) | set(wide[1:]) | set(deep[1:]))
    barrier = pltpu.get_barrier_semaphore()
    for mask in peers:
        pl.semaphore_signal(
            barrier, inc=1, device_id={"rows": flip_bits(me, mask)}, device_id_type=MESH
        )
    pl.semaphore_signal(barrier, inc=1, device_id={"cols": 1 - col}, device_id_type=MESH)

    loads = [
        pltpu.make_async_copy(here, there, load_sem.at[i])
        for i, (here, there) in enumerate(
            [
                (size_hbm, size_ref),
                (feat_hbm, feat),
                (src_hbm, src_ref),
                (dst_hbm, dst_ref),
                (weight_hbm, weights.at[0]),
                (bias_hbm, biases.at[0]),
                (gout_hbm, gouts.at[0]),
            ]
        )
    ]
    tile_loads = [
        pltpu.make_async_copy(
            tiles_hbm.at[pl.ds(i * part_slots, part_slots)],
            tiles.at[pl.ds(i * part_slots, part_slots)],
            tile_sem.at[i],
        )
        for i in range(parts)
    ]
    for load in loads + tile_loads:
        load.start()

    loads[0].wait()
    loads[1].wait()
    node_lane = lax.broadcasted_iota(jnp.int32, (half, nodes), 1)
    live = node_lane < jnp.where(node_lane < tall, size_ref[0], size_ref[1] + tall)
    packed[levels] = jnp.where(live, feat[...].astype(F32), 0.0).astype(BF16)

    clusters = []
    for k in range(levels + 1):
        group = flip_bits(me, near[k]) if k < levels else me
        clusters += [group * 2, group * 2 + 1]
    for load in loads[2:4]:
        load.wait()
    count = count_ref[0]

    def one_tile(t, carried):
        first, second, prev, lasts = carried
        src = src_ref[t]
        used = t < count
        keep = (src == prev) & used
        to_second = dst_ref[t] == 1
        tile = tiles[t].astype(F32)
        zero = jnp.zeros_like(tile)
        first = jnp.where(keep, first, zero) + jnp.where(used & (~to_second), tile, zero)
        second = jnp.where(keep, second, zero) + jnp.where(used & to_second, tile, zero)
        sums[0, t] = first.astype(BF16)
        sums[1, t] = second.astype(BF16)
        lasts = tuple(
            jnp.where(used & (src == cluster), t, last)
            for last, cluster in zip(lasts, clusters)
        )
        return first, second, src, lasts

    blank = jnp.zeros((tall, tall), F32)
    running = (blank, blank, jnp.int32(-1), tuple(jnp.int32(-1) for _ in clusters))
    for i in range(early):
        tile_loads[i].wait()
        running = lax.fori_loop(i * part_slots, (i + 1) * part_slots, one_tile, running)

    pl.semaphore_wait(barrier, len(peers) + 1)

    feature_copies = [
        remote(packed.at[levels], packed.at[k], x_send.at[k], x_recv.at[k], near[k])
        for k in range(levels)
    ]
    for copy in feature_copies[::-1]:
        copy.start()
    side_copies = [
        remote(weight_hbm, weights.at[1], p_send.at[0], p_recv.at[0], None),
        remote(bias_hbm, biases.at[1], p_send.at[1], p_recv.at[1], None),
        remote(gout_hbm, gouts.at[1], p_send.at[2], p_recv.at[2], None),
    ]
    for copy in side_copies:
        copy.start()

    for i in range(early, parts):
        tile_loads[i].wait()
        running = lax.fori_loop(i * part_slots, (i + 1) * part_slots, one_tile, running)
    for j, last in enumerate(running[3]):
        at = jnp.maximum(last, 0)
        for d in range(2):
            block = sums[d, at]
            dense[j // 2, d * tall : (d + 1) * tall, (j % 2) * tall : (j % 2 + 1) * tall] = (
                jnp.where(last >= 0, block, jnp.zeros_like(block))
            )

    def turn(side):
        turned[side] = weights[side].astype(F32).T.astype(BF16)
        gout_turned[side] = gouts[side].astype(F32).T.astype(BF16)
        bias_turned[side] = jnp.broadcast_to(biases[side], (tall, biases.shape[2])).T

    for load in loads[4:]:
        load.wait()
    turn(0)

    by_lanes = (((1,), (1,)), ((), ()))
    total = None
    for k in [levels] + list(range(levels)):
        if k < levels:
            feature_copies[k].wait_recv()
        term = lax.dot_general(packed[k], dense[k], by_lanes, preferred_element_type=F32)
        total = term if total is None else total + term
    own_rows = pl.ds(pl.multiple_of(col * half, half), half)
    agg[own_rows, :] = total.astype(BF16)
    agg_copy = remote(
        agg.at[own_rows, :], agg.at[own_rows, :], p_send.at[3], p_recv.at[3], None
    )
    agg_copy.start()
    for copy in side_copies:
        copy.wait_recv()
    turn(1)
    other_rows = pl.ds(pl.multiple_of((1 - col) * half, half), half)
    remote(
        agg.at[own_rows, :], agg.at[other_rows, :], p_send.at[3], p_recv.at[3], None
    ).wait_recv()

    agg_all = agg[...]
    node_lane = lax.broadcasted_iota(jnp.int32, (turned.shape[1], nodes), 1)
    live_all = node_lane < jnp.where(node_lane < tall, size_ref[0], size_ref[1] + tall)
    grads = []
    hidden = None
    for side in range(2):
        pre = jnp.dot(turned[side], agg_all, preferred_element_type=F32)
        pre = pre + jnp.concatenate([bias_turned[side]] * (nodes // tall), axis=1)
        gate = jax.nn.sigmoid(pre)
        if side == 0:
            hidden = jnp.where(live_all, pre * gate, 0.0)
        grad = gout_turned[side].astype(F32) * gate * (1.0 + pre * (1.0 - gate))
        grads.append(jnp.where(live_all, grad, 0.0).astype(BF16))

    ones = jnp.ones((16, nodes), BF16)
    grad_weight = lax.dot_general(
        jnp.concatenate([agg_all, ones], axis=0),
        grads[0],
        by_lanes,
        preferred_element_type=F32,
    )
    wide_feat, units = gw_ref.shape
    chunk = wide_feat // wide_count
    for j in range(wide_count):
        stage[j, :chunk, :] = grad_weight[j * chunk : (j + 1) * chunk]
        stage[j, chunk:, :] = grad_weight[wide_feat : wide_feat + 8]

    my_wide, my_deep = place(me, wide), place(me, deep)
    scatter_copies = [
        remote(
            stage.at[place(flip_bits(me, wide[m]), wide)],
            fold_in.at[my_wide],
            r1_send.at[m],
            r1_recv.at[m],
            wide[m],
        )
        for m in range(1, wide_count)
    ]
    for copy in scatter_copies:
        copy.start()
    fold_in[my_wide] = stage[my_wide]

    grad_agg = sum(
        jnp.dot(weights[side, own_rows, :], grads[side], preferred_element_type=F32)
        for side in range(2)
    ).astype(BF16)
    back_copies = [
        remote(give.at[k], take.at[k], c_send.at[k], c_recv.at[k], near[k])
        for k in range(levels)
    ]
    for k in range(levels - 1, -1, -1):
        give[k] = jnp.dot(grad_agg, dense[k], preferred_element_type=F32).astype(BF16)
        back_copies[k].start()
    own_back[...] = jnp.dot(grad_agg, dense[levels], preferred_element_type=F32)
    hidden_ref[...] = hidden.T.astype(BF16)

    for m in range(1, wide_count):
        remote(
            stage.at[0],
            fold_in.at[place(flip_bits(me, wide[m]), wide)],
            r1_send.at[m],
            r1_recv.at[m],
            wide[m],
        ).wait_recv()
    part = fold_in[0]
    for m in range(1, wide_count):
        part = part + fold_in[m]
    fold_mid[my_deep] = part
    deep_copies = [
        remote(
            fold_mid.at[my_deep], fold_mid.at[my_deep], r2_send.at[m], r2_recv.at[m], deep[m]
        )
        for m in range(1, deep_count)
    ]
    for copy in deep_copies:
        copy.start()

    back = own_back[...]
    for k in range(levels):
        back_copies[k].wait_recv()
        back = back + take[k].astype(F32)
    gf_ref[...] = jnp.where(live, back, 0.0).astype(BF16)

    for m in range(1, deep_count):
        remote(
            fold_mid.at[my_deep],
            fold_mid.at[place(flip_bits(me, deep[m]), deep)],
            r2_send.at[m],
            r2_recv.at[m],
            deep[m],
        ).wait_recv()
    part = fold_mid[0]
    for m in range(1, deep_count):
        part = part + fold_mid[m]
    part = part * scale
    gb_ref[...] = part[chunk : chunk + 1, :]
    fold_all[my_wide] = part[:chunk]
    gather_copies = [
        remote(
            fold_all.at[my_wide], fold_all.at[my_wide], r3_send.at[m], r3_recv.at[m], wide[m]
        )
        for m in range(1, wide_count)
    ]
    for copy in gather_copies:
        copy.start()
    for m in range(1, wide_count):
        remote(
            fold_all.at[my_wide],
            fold_all.at[place(flip_bits(me, wide[m]), wide)],
            r3_send.at[m],
            r3_recv.at[m],
            wide[m],
        ).wait_recv()
    gw_ref[...] = fold_all[...].reshape(gw_ref.shape)

    for copy in (
        feature_copies
        + side_copies
        + [agg_copy]
        + scatter_copies
        + back_copies
        + deep_copies
        + gather_copies
    ):
        copy.wait_send()


def write_kernel(*refs):
    count = (len(refs) - 1) // 2
    sem = refs[-1]
    copies = [
        pltpu.make_async_copy(refs[i], refs[count + i], sem.at[i]) for i in range(count)
    ]
    for copy in copies:
        copy.start()
    for copy in copies:
        copy.wait()


def group_masks(bits):
    return [
        sum(1 << bit for place, bit in enumerate(bits) if m >> place & 1)
        for m in range(1 << len(bits))
    ]


def solution(mesh):
    row_groups = mesh.shape["rows"]
    levels = row_groups.bit_length() - 1
    deep_bits = [bit for bit in range(levels) if 1 <= bit <= (3 if levels > 4 else 1)]
    wide_bits = [bit for bit in range(levels) if bit not in deep_bits]
    near = [1 << bit for bit in range(levels)]
    wide, deep = group_masks(wide_bits), group_masks(deep_bits)

    def local(
        features, adj_tiles, tile_src, tile_dst, tile_count, cluster_size, weight, bias, grad_out
    ):
        slots, tall, _ = adj_tiles.shape
        nodes, half = features.shape
        wide_feat, units = weight.shape
        chunk = wide_feat // len(wide)
        dma = pltpu.SemaphoreType.DMA
        plan = (near, wide, deep, 1.0 / math.sqrt(nodes * row_groups), EARLY)
        shapes = [
            ((nodes, units), BF16),
            ((wide_feat, units), F32),
            ((1, units), F32),
            ((half, nodes), BF16),
        ]
        inputs = [
            tile_src,
            tile_dst,
            tile_count,
            cluster_size,
            features.T,
            adj_tiles,
            weight,
            bias.reshape(1, units),
            grad_out,
        ]
        results = pl.pallas_call(
            functools.partial(layer_kernel, plan),
            out_shape=tuple(pltpu.VMEM(shape, kind) for shape, kind in shapes),
            in_specs=[
                pl.BlockSpec(memory_space=pltpu.SMEM if x is tile_count else pltpu.HBM)
                for x in inputs
            ],
            out_specs=(pl.BlockSpec(memory_space=pltpu.VMEM),) * len(shapes),
            scratch_shapes=[
                pltpu.SMEM((slots,), jnp.int32),
                pltpu.SMEM((slots,), jnp.int32),
                pltpu.SMEM((2,), jnp.int32),
                pltpu.VMEM((half, nodes), BF16),
                pltpu.VMEM((slots, tall, tall), BF16),
                pltpu.VMEM((2, wide_feat, units), BF16),
                pltpu.VMEM((2, 1, units), F32),
                pltpu.VMEM((2, nodes, units), BF16),
                pltpu.VMEM((levels + 1, half, nodes), BF16),
                pltpu.VMEM((2, slots, tall, tall), BF16),
                pltpu.VMEM((levels + 1, nodes, nodes), BF16),
                pltpu.VMEM((wide_feat, nodes), BF16),
                pltpu.VMEM((2, units, wide_feat), BF16),
                pltpu.VMEM((2, units, nodes), BF16),
                pltpu.VMEM((2, units, tall), F32),
                pltpu.VMEM((len(wide), chunk + 8, units), F32),
                pltpu.VMEM((len(wide), chunk + 8, units), F32),
                pltpu.VMEM((len(deep), chunk + 8, units), F32),
                pltpu.VMEM((len(wide), chunk, units), F32),
                pltpu.VMEM((levels, half, nodes), BF16),
                pltpu.VMEM((levels, half, nodes), BF16),
                pltpu.VMEM((half, nodes), F32),
                dma((7,)),
                dma((4,)),
                dma((levels,)),
                dma((levels,)),
                dma((4,)),
                dma((4,)),
                dma((levels,)),
                dma((levels,)),
                dma((len(wide),)),
                dma((len(wide),)),
                dma((len(deep),)),
                dma((len(deep),)),
                dma((len(wide),)),
                dma((len(wide),)),
            ],
            compiler_params=pltpu.CompilerParams(
                collective_id=0, has_side_effects=True, vmem_limit_bytes=40 * 1024 * 1024
            ),
            name="graph_layer",
        )(
            *[
                x if x is tile_count else pltpu.with_memory_space_constraint(x, pltpu.HBM)
                for x in inputs
            ]
        )
        hidden, grad_weight, grad_bias, grad_features = pl.pallas_call(
            write_kernel,
            out_shape=tuple(pltpu.HBM(shape, kind) for shape, kind in shapes),
            in_specs=[pl.BlockSpec(memory_space=pltpu.VMEM)] * len(shapes),
            out_specs=(pl.BlockSpec(memory_space=pltpu.HBM),) * len(shapes),
            scratch_shapes=[dma((len(shapes),))],
            name="write_results",
        )(*[pltpu.with_memory_space_constraint(x, pltpu.VMEM) for x in results])
        return hidden, grad_weight, grad_bias.reshape(units), grad_features.T

    return jax.shard_map(
        local,
        mesh=mesh,
        in_specs=(
            P("rows", "cols"),
            P("rows", None, None),
            P("rows"),
            P("rows"),
            P("rows"),
            P("rows"),
            P(None, "cols"),
            P("cols"),
            P("rows", "cols"),
        ),
        out_specs=(P("rows", "cols"), P(None, "cols"), P("cols"), P("rows", "cols")),
        check_vma=False,
    )
```

```python
import functools
import math

import jax
import jax.numpy as jnp
from jax import lax
from jax.experimental import pallas as pl
from jax.experimental.pallas import tpu as pltpu
from jax.sharding import PartitionSpec as P

F32 = jnp.float32
BF16 = jnp.bfloat16
MESH = pl.DeviceIdType.MESH
PARTS = 4
MID = jnp.bfloat16
RELAY = 0


class Spot:
    def __init__(self, index, levels):
        self.index = index
        self.levels = levels
        self.bits = [lax.rem(lax.div(index, jnp.int32(1 << b)), jnp.int32(2)) for b in range(levels)]

    def flipped(self, mask):
        out = self.index
        for b in range(self.levels):
            if mask >> b & 1:
                out = out + ((1 << b) - (2 << b) * self.bits[b])
        return out

    def place(self, masks, mask=0):
        out = jnp.int32(0)
        for p in range(len(masks).bit_length() - 1):
            bit = self.bits[masks[1 << p].bit_length() - 1]
            out = out + (1 << p) * (1 - bit if masks[1 << p] & mask else bit)
        return out


def reach(mask):
    z, y, x = mask >> 1 & 7, mask >> 4 & 3, mask >> 6
    far_z = max(min(abs((a ^ z) - a), 8 - abs((a ^ z) - a)) for a in range(8))
    far_y = max(min(abs((a ^ y) - a), 4 - abs((a ^ y) - a)) for a in range(4))
    return far_z + far_y + x


def layer_kernel(
    plan,
    src_hbm,
    dst_hbm,
    count_ref,
    size_hbm,
    feat_hbm,
    tiles_hbm,
    weight_hbm,
    bias_hbm,
    gout_hbm,
    hidden_ref,
    gw_ref,
    gb_ref,
    gf_ref,
    src_ref,
    dst_ref,
    size_ref,
    feat,
    tiles,
    weights,
    biases,
    gouts,
    packed,
    sums,
    dense,
    turned,
    gout_turned,
    part_back,
    part_in,
    stage,
    fold_in,
    fold_mid,
    fold_all,
    bias_in,
    bias_mid,
    give,
    take,
    own_back,
    load_sem,
    tile_sem,
    x_send,
    x_recv,
    y_send,
    y_recv,
    p_send,
    p_recv,
    c_send,
    c_recv,
    r1_send,
    r1_recv,
    r2_send,
    r2_recv,
    r3_send,
    r3_recv,
    b1_send,
    b1_recv,
    b2_send,
    b2_recv,
):
    near, wide, deep, scale = plan
    levels = len(near)
    wide_count, deep_count = len(wide), len(deep)
    me = Spot(lax.axis_index("rows"), levels)
    col = lax.axis_index("cols")
    slots, tall, _ = tiles.shape
    half, nodes = feat.shape
    own_rows = pl.ds(pl.multiple_of(col * half, half), half)
    other_rows = pl.ds(pl.multiple_of((1 - col) * half, half), half)
    relayed = [k for k in range(levels) if reach(near[k]) <= RELAY]
    across = [k for k in range(levels + 1) if k not in relayed]
    far_near = sorted(range(levels), key=lambda k: -reach(near[k]))
    far_wide = sorted(range(1, wide_count), key=lambda m: -reach(wide[m]))
    far_deep = sorted(range(1, deep_count), key=lambda m: -reach(deep[m]))
    parts = tile_sem.shape[0]
    part_slots = slots // parts

    def remote(src, dst, send, recv, mask, crossing=False):
        who = {"rows": me.flipped(mask)} if mask else {}
        if crossing:
            who["cols"] = 1 - col
        return pltpu.make_async_remote_copy(
            src_ref=src,
            dst_ref=dst,
            send_sem=send,
            recv_sem=recv,
            device_id=who,
            device_id_type=MESH,
        )

    peers = [(mask, False) for mask in set(near) | set(wide[1:]) | set(deep[1:])]
    peers += [(near[k] if k < levels else 0, True) for k in across]
    peers.sort(key=lambda peer: -reach(peer[0]) - 2 * peer[1])
    barrier = pltpu.get_barrier_semaphore()
    for mask, crossing in peers:
        who = {"rows": me.flipped(mask)} if mask else {}
        if crossing:
            who["cols"] = 1 - col
        pl.semaphore_signal(barrier, inc=1, device_id=who, device_id_type=MESH)

    loads = [
        pltpu.make_async_copy(here, there, load_sem.at[i])
        for i, (here, there) in enumerate(
            [
                (size_hbm, size_ref),
                (feat_hbm, feat),
                (src_hbm, src_ref),
                (dst_hbm, dst_ref),
                (weight_hbm, weights),
                (bias_hbm, biases),
                (gout_hbm, gouts),
            ]
        )
    ]
    tile_loads = [
        pltpu.make_async_copy(
            tiles_hbm.at[pl.ds(i * part_slots, part_slots)],
            tiles.at[pl.ds(i * part_slots, part_slots)],
            tile_sem.at[i],
        )
        for i in range(parts)
    ]
    for load in loads + tile_loads:
        load.start()

    loads[0].wait()
    loads[1].wait()
    node_lane = lax.broadcasted_iota(jnp.int32, (half, nodes), 1)
    live = node_lane < jnp.where(node_lane < tall, size_ref[0], size_ref[1] + tall)
    packed[levels, own_rows, :] = jnp.where(live, feat[...].astype(F32), 0.0).astype(BF16)

    clusters = []
    for k in range(levels + 1):
        group = me.flipped(near[k]) if k < levels else me.index
        clusters += [group * 2, group * 2 + 1]
    for load in loads[2:4]:
        load.wait()
    count = count_ref[0]

    def one_tile(t, carried):
        first, second, prev, lasts = carried
        src = src_ref[t]
        used = t < count
        keep = (src == prev) & used
        to_second = dst_ref[t] == 1
        tile = tiles[t].astype(F32)
        zero = jnp.zeros_like(tile)
        first = jnp.where(keep, first, zero) + jnp.where(used & (~to_second), tile, zero)
        second = jnp.where(keep, second, zero) + jnp.where(used & to_second, tile, zero)
        sums[0, t] = first.astype(BF16)
        sums[1, t] = second.astype(BF16)
        lasts = tuple(
            jnp.where(used & (src == cluster), t, last)
            for last, cluster in zip(lasts, clusters)
        )
        return first, second, src, lasts

    blank = jnp.zeros((tall, tall), F32)
    running = (blank, blank, jnp.int32(-1), tuple(jnp.int32(-1) for _ in clusters))
    pl.semaphore_wait(barrier, len(peers))

    mine = packed.at[levels, own_rows, :]
    feature_copies = {
        (k, crossing): remote(
            mine,
            packed.at[k, own_rows, :],
            (y_send if crossing else x_send).at[k],
            (y_recv if crossing else x_recv).at[k],
            near[k] if k < levels else 0,
            crossing,
        )
        for crossing in (True, False)
        for k in (across if crossing else range(levels))
    }
    feature_order = sorted(
        feature_copies,
        key=lambda c: -(reach(near[c[0]]) if c[0] < levels else 9) - 2 * c[1],
    )
    for c in feature_order:
        feature_copies[c].start()

    for i in range(parts):
        tile_loads[i].wait()
        running = lax.fori_loop(i * part_slots, (i + 1) * part_slots, one_tile, running)
    theirs = packed.at[levels, other_rows, :]
    relays = [
        remote(theirs, packed.at[k, other_rows, :], y_send.at[k], y_recv.at[k], near[k])
        for k in relayed
    ]
    if relayed:
        remote(
            mine, theirs, y_send.at[levels], y_recv.at[levels], near[0], True
        ).wait_recv()
    for copy in relays:
        copy.start()

    for j, last in enumerate(running[3]):
        at = jnp.maximum(last, 0)
        for d in range(2):
            block = sums[d, at]
            dense[j // 2, d * tall : (d + 1) * tall, (j % 2) * tall : (j % 2 + 1) * tall] = (
                jnp.where(last >= 0, block, jnp.zeros_like(block))
            )

    for load in loads[4:]:
        load.wait()
    turned[...] = weights[...].astype(F32).T.astype(BF16)
    gout_turned[...] = gouts[...].astype(F32).T
    bias_turned = jnp.broadcast_to(biases[...], (tall, biases.shape[1])).T

    by_lanes = (((1,), (1,)), ((), ()))
    total = None
    for k in [levels] + far_near[::-1]:
        if k < levels:
            feature_copies[k, False].wait_recv()
        if k < levels or not relayed:
            remote(
                mine, packed.at[k, other_rows, :], y_send.at[k], y_recv.at[k], near[0], True
            ).wait_recv()
        term = lax.dot_general(packed[k], dense[k], by_lanes, preferred_element_type=F32)
        total = term if total is None else total + term
    agg_all = total.astype(BF16)

    node_lane = lax.broadcasted_iota(jnp.int32, (turned.shape[0], nodes), 1)
    live_all = node_lane < jnp.where(node_lane < tall, size_ref[0], size_ref[1] + tall)
    pre = jnp.dot(turned[...], agg_all, preferred_element_type=F32)
    pre = pre + jnp.concatenate([bias_turned] * (nodes // tall), axis=1)
    gate = jax.nn.sigmoid(pre)
    hidden = jnp.where(live_all, pre * gate, 0.0)
    grad = gout_turned[...] * gate * (1.0 + pre * (1.0 - gate))
    grad = jnp.where(live_all, grad, 0.0).astype(BF16)

    ones = jnp.ones((16, nodes), BF16)
    grad_weight = lax.dot_general(
        jnp.concatenate([agg_all, ones], axis=0),
        grad,
        by_lanes,
        preferred_element_type=F32,
    )
    wide_feat, units = gw_ref.shape
    chunk = wide_feat // wide_count
    for j in range(wide_count):
        stage[j] = grad_weight[j * chunk : (j + 1) * chunk]
    my_wide, my_deep = me.place(wide), me.place(deep)
    bias_in[my_wide] = grad_weight[wide_feat : wide_feat + 1]
    scatter_copies, bias_copies = [], []
    for m in far_wide:
        scatter_copies.append(
            remote(
                stage.at[me.place(wide, wide[m])],
                fold_in.at[my_wide],
                r1_send.at[m],
                r1_recv.at[m],
                wide[m],
            )
        )
        bias_copies.append(
            remote(
                bias_in.at[my_wide],
                bias_in.at[my_wide],
                b1_send.at[m],
                b1_recv.at[m],
                wide[m],
            )
        )
        scatter_copies[-1].start()
        bias_copies[-1].start()
    fold_in[my_wide] = stage[my_wide]

    part_back[...] = jnp.dot(weights[...], grad, preferred_element_type=F32)
    half_copy = remote(
        part_back.at[other_rows, :], part_in, p_send.at[0], p_recv.at[0], 0, True
    )
    half_copy.start()
    hidden_ref[...] = hidden.T.astype(BF16)

    for m in far_wide[::-1]:
        there = me.place(wide, wide[m])
        remote(
            stage.at[0], fold_in.at[there], r1_send.at[m], r1_recv.at[m], wide[m]
        ).wait_recv()
        remote(
            bias_in.at[there], bias_in.at[there], b1_send.at[m], b1_recv.at[m], wide[m]
        ).wait_recv()
    part, bias_part = fold_in[0], bias_in[0]
    for m in range(1, wide_count):
        part, bias_part = part + fold_in[m], bias_part + bias_in[m]
    fold_mid[my_deep] = part.astype(fold_mid.dtype)
    bias_mid[my_deep] = bias_part
    deep_copies = []
    for m in far_deep:
        for fold, send, recv in ((fold_mid, r2_send, r2_recv), (bias_mid, b2_send, b2_recv)):
            deep_copies.append(
                remote(fold.at[my_deep], fold.at[my_deep], send.at[m], recv.at[m], deep[m])
            )
            deep_copies[-1].start()

    half_copy.wait_recv()
    grad_agg = (part_back[own_rows, :] + part_in[...]).astype(BF16)
    back_copies = [
        remote(give.at[k], take.at[k], c_send.at[k], c_recv.at[k], near[k])
        for k in range(levels)
    ]
    for k in far_near[::-1]:
        give[k] = jnp.dot(grad_agg, dense[k], preferred_element_type=F32).astype(BF16)
        back_copies[k].start()
    own_back[...] = jnp.dot(grad_agg, dense[levels], preferred_element_type=F32)

    for m in far_deep[::-1]:
        there = me.place(deep, deep[m])
        for fold, send, recv in ((fold_mid, r2_send, r2_recv), (bias_mid, b2_send, b2_recv)):
            remote(
                fold.at[there], fold.at[there], send.at[m], recv.at[m], deep[m]
            ).wait_recv()
    part, bias_part = fold_mid[0].astype(F32), bias_mid[0]
    for m in range(1, deep_count):
        part, bias_part = part + fold_mid[m].astype(F32), bias_part + bias_mid[m]
    fold_all[my_wide] = part * scale
    gather_copies = [
        remote(
            fold_all.at[my_wide], fold_all.at[my_wide], r3_send.at[m], r3_recv.at[m], wide[m]
        )
        for m in far_wide
    ]
    for copy in gather_copies:
        copy.start()
    gb_ref[...] = bias_part * scale

    back = own_back[...]
    for k in far_near[::-1]:
        back_copies[k].wait_recv()
        back = back + take[k].astype(F32)
    gf_ref[...] = jnp.where(live, back, 0.0).astype(BF16)

    for m in far_wide[::-1]:
        remote(
            fold_all.at[my_wide],
            fold_all.at[me.place(wide, wide[m])],
            r3_send.at[m],
            r3_recv.at[m],
            wide[m],
        ).wait_recv()
    gw_ref[...] = fold_all[...].reshape(gw_ref.shape)

    for copy in (
        list(feature_copies.values())
        + relays
        + scatter_copies
        + bias_copies
        + [half_copy]
        + back_copies
        + deep_copies
        + gather_copies
    ):
        copy.wait_send()


def write_kernel(*refs):
    count = (len(refs) - 1) // 2
    sem = refs[-1]
    copies = [
        pltpu.make_async_copy(refs[i], refs[count + i], sem.at[i]) for i in range(count)
    ]
    for copy in copies:
        copy.start()
    for copy in copies:
        copy.wait()


def group_masks(bits):
    return [
        sum(1 << bit for place, bit in enumerate(bits) if m >> place & 1)
        for m in range(1 << len(bits))
    ]


def solution(mesh):
    row_groups = mesh.shape["rows"]
    levels = row_groups.bit_length() - 1
    wide_bits = [bit for bit in range(levels) if bit in (0, 4, 5)]
    deep_bits = [bit for bit in range(levels) if bit not in wide_bits]
    near = [1 << bit for bit in range(levels)]
    wide, deep = group_masks(wide_bits), group_masks(deep_bits)

    def local(
        features, adj_tiles, tile_src, tile_dst, tile_count, cluster_size, weight, bias, grad_out
    ):
        slots, tall, _ = adj_tiles.shape
        nodes, half = features.shape
        wide_feat, units = weight.shape
        chunk = wide_feat // len(wide)
        dma = pltpu.SemaphoreType.DMA
        plan = (near, wide, deep, 1.0 / math.sqrt(nodes * row_groups))
        shapes = [
            ((nodes, units), BF16),
            ((wide_feat, units), F32),
            ((1, units), F32),
            ((half, nodes), BF16),
        ]
        inputs = [
            tile_src,
            tile_dst,
            tile_count,
            cluster_size,
            features.T,
            adj_tiles,
            weight,
            bias.reshape(1, units),
            grad_out,
        ]
        results = pl.pallas_call(
            functools.partial(layer_kernel, plan),
            out_shape=tuple(pltpu.VMEM(shape, kind) for shape, kind in shapes),
            in_specs=[
                pl.BlockSpec(memory_space=pltpu.SMEM if x is tile_count else pltpu.HBM)
                for x in inputs
            ],
            out_specs=(pl.BlockSpec(memory_space=pltpu.VMEM),) * len(shapes),
            scratch_shapes=[
                pltpu.SMEM((slots,), jnp.int32),
                pltpu.SMEM((slots,), jnp.int32),
                pltpu.SMEM((2,), jnp.int32),
                pltpu.VMEM((half, nodes), BF16),
                pltpu.VMEM((slots, tall, tall), BF16),
                pltpu.VMEM((wide_feat, units), BF16),
                pltpu.VMEM((1, units), F32),
                pltpu.VMEM((nodes, units), BF16),
                pltpu.VMEM((levels + 1, wide_feat, nodes), BF16),
                pltpu.VMEM((2, slots, tall, tall), BF16),
                pltpu.VMEM((levels + 1, nodes, nodes), BF16),
                pltpu.VMEM((units, wide_feat), BF16),
                pltpu.VMEM((units, nodes), F32),
                pltpu.VMEM((wide_feat, nodes), F32),
                pltpu.VMEM((half, nodes), F32),
                pltpu.VMEM((len(wide), chunk, units), F32),
                pltpu.VMEM((len(wide), chunk, units), F32),
                pltpu.VMEM((len(deep), chunk, units), MID),
                pltpu.VMEM((len(wide), chunk, units), F32),
                pltpu.VMEM((len(wide), 1, units), F32),
                pltpu.VMEM((len(deep), 1, units), F32),
                pltpu.VMEM((levels, half, nodes), BF16),
                pltpu.VMEM((levels, half, nodes), BF16),
                pltpu.VMEM((half, nodes), F32),
                dma((7,)),
                dma((PARTS,)),
                dma((levels,)),
                dma((levels,)),
                dma((levels + 1,)),
                dma((levels + 1,)),
                dma((1,)),
                dma((1,)),
                dma((levels,)),
                dma((levels,)),
                dma((len(wide),)),
                dma((len(wide),)),
                dma((len(deep),)),
                dma((len(deep),)),
                dma((len(wide),)),
                dma((len(wide),)),
                dma((len(wide),)),
                dma((len(wide),)),
                dma((len(deep),)),
                dma((len(deep),)),
            ],
            compiler_params=pltpu.CompilerParams(
                collective_id=0, has_side_effects=True, vmem_limit_bytes=40 * 1024 * 1024
            ),
            name="graph_layer",
        )(
            *[
                x if x is tile_count else pltpu.with_memory_space_constraint(x, pltpu.HBM)
                for x in inputs
            ]
        )
        hidden, grad_weight, grad_bias, grad_features = pl.pallas_call(
            write_kernel,
            out_shape=tuple(pltpu.HBM(shape, kind) for shape, kind in shapes),
            in_specs=[pl.BlockSpec(memory_space=pltpu.VMEM)] * len(shapes),
            out_specs=(pl.BlockSpec(memory_space=pltpu.HBM),) * len(shapes),
            scratch_shapes=[dma((len(shapes),))],
            name="write_results",
        )(*[pltpu.with_memory_space_constraint(x, pltpu.VMEM) for x in results])
        return hidden, grad_weight, grad_bias.reshape(units), grad_features.T

    return jax.shard_map(
        local,
        mesh=mesh,
        in_specs=(
            P("rows", "cols"),
            P("rows", None, None),
            P("rows"),
            P("rows"),
            P("rows"),
            P("rows"),
            P(None, "cols"),
            P("cols"),
            P("rows", "cols"),
        ),
        out_specs=(P("rows", "cols"), P(None, "cols"), P("cols"), P("rows", "cols")),
        check_vma=False,
    )
```

```python
import functools
import math

import jax
import jax.numpy as jnp
from jax import lax
from jax.experimental import pallas as pl
from jax.experimental.pallas import tpu as pltpu
from jax.sharding import PartitionSpec as P

F32 = jnp.float32
BF16 = jnp.bfloat16
MESH = pl.DeviceIdType.MESH
PARTS = 4
MID = jnp.bfloat16
RELAY = 0


class Spot:
    def __init__(self, index, levels):
        self.index = index
        self.levels = levels
        self.bits = [lax.rem(lax.div(index, jnp.int32(1 << b)), jnp.int32(2)) for b in range(levels)]

    def flipped(self, mask):
        out = self.index
        for b in range(self.levels):
            if mask >> b & 1:
                out = out + ((1 << b) - (2 << b) * self.bits[b])
        return out

    def place(self, masks, mask=0):
        out = jnp.int32(0)
        for p in range(len(masks).bit_length() - 1):
            bit = self.bits[masks[1 << p].bit_length() - 1]
            out = out + (1 << p) * (1 - bit if masks[1 << p] & mask else bit)
        return out


def reach(mask):
    z, y, x = mask >> 1 & 7, mask >> 4 & 3, mask >> 6
    far_z = max(min(abs((a ^ z) - a), 8 - abs((a ^ z) - a)) for a in range(8))
    far_y = max(min(abs((a ^ y) - a), 4 - abs((a ^ y) - a)) for a in range(4))
    return far_z + far_y + x


def layer_kernel(
    plan,
    src_hbm,
    dst_hbm,
    count_ref,
    size_hbm,
    feat_hbm,
    tiles_hbm,
    weight_hbm,
    bias_hbm,
    gout_hbm,
    hidden_ref,
    gw_ref,
    gb_ref,
    gf_ref,
    src_ref,
    dst_ref,
    size_ref,
    feat,
    tiles,
    weights,
    biases,
    gouts,
    packed,
    sums,
    dense,
    turned,
    gout_turned,
    part_back,
    part_in,
    stage,
    fold_in,
    fold_mid,
    fold_all,
    bias_mid,
    give,
    take,
    own_back,
    load_sem,
    tile_sem,
    x_send,
    x_recv,
    y_send,
    y_recv,
    p_send,
    p_recv,
    c_send,
    c_recv,
    r1_send,
    r1_recv,
    r2_send,
    r2_recv,
    r3_send,
    r3_recv,
    b2_send,
    b2_recv,
):
    near, wide, deep, scale = plan
    levels = len(near)
    wide_count, deep_count = len(wide), len(deep)
    me = Spot(lax.axis_index("rows"), levels)
    col = lax.axis_index("cols")
    slots, tall, _ = tiles.shape
    half, nodes = feat.shape
    own_rows = pl.ds(pl.multiple_of(col * half, half), half)
    other_rows = pl.ds(pl.multiple_of((1 - col) * half, half), half)
    relayed = [k for k in range(levels) if reach(near[k]) <= RELAY]
    across = [k for k in range(levels + 1) if k not in relayed]
    far_near = sorted(range(levels), key=lambda k: -reach(near[k]))
    far_wide = sorted(range(1, wide_count), key=lambda m: -reach(wide[m]))
    far_deep = sorted(range(1, deep_count), key=lambda m: (-(deep[m] & 8), -reach(deep[m])))
    parts = tile_sem.shape[0]
    part_slots = slots // parts

    def remote(src, dst, send, recv, mask, crossing=False):
        who = {"rows": me.flipped(mask)} if mask else {}
        if crossing:
            who["cols"] = 1 - col
        return pltpu.make_async_remote_copy(
            src_ref=src,
            dst_ref=dst,
            send_sem=send,
            recv_sem=recv,
            device_id=who,
            device_id_type=MESH,
        )

    peers = [(mask, False) for mask in set(near) | set(wide[1:]) | set(deep[1:])]
    peers += [(near[k] if k < levels else 0, True) for k in across]
    peers.sort(key=lambda peer: -reach(peer[0]) - 2 * peer[1])
    barrier = pltpu.get_barrier_semaphore()
    for mask, crossing in peers:
        who = {"rows": me.flipped(mask)} if mask else {}
        if crossing:
            who["cols"] = 1 - col
        pl.semaphore_signal(barrier, inc=1, device_id=who, device_id_type=MESH)

    loads = [
        pltpu.make_async_copy(here, there, load_sem.at[i])
        for i, (here, there) in enumerate(
            [
                (size_hbm, size_ref),
                (feat_hbm, feat),
                (src_hbm, src_ref),
                (dst_hbm, dst_ref),
                (weight_hbm, weights),
                (bias_hbm, biases),
                (gout_hbm, gouts),
            ]
        )
    ]
    tile_loads = [
        pltpu.make_async_copy(
            tiles_hbm.at[pl.ds(i * part_slots, part_slots)],
            tiles.at[pl.ds(i * part_slots, part_slots)],
            tile_sem.at[i],
        )
        for i in range(parts)
    ]
    for load in loads + tile_loads:
        load.start()

    loads[0].wait()
    loads[1].wait()
    node_lane = lax.broadcasted_iota(jnp.int32, (half, nodes), 1)
    live = node_lane < jnp.where(node_lane < tall, size_ref[0], size_ref[1] + tall)
    packed[levels, own_rows, :] = jnp.where(live, feat[...].astype(F32), 0.0).astype(BF16)

    clusters = []
    for k in range(levels + 1):
        group = me.flipped(near[k]) if k < levels else me.index
        clusters += [group * 2, group * 2 + 1]
    for load in loads[2:4]:
        load.wait()
    count = count_ref[0]

    def one_tile(t, carried):
        first, second, prev, lasts = carried
        src = src_ref[t]
        used = t < count
        keep = (src == prev) & used
        to_second = dst_ref[t] == 1
        tile = tiles[t].astype(F32)
        zero = jnp.zeros_like(tile)
        first = jnp.where(keep, first, zero) + jnp.where(used & (~to_second), tile, zero)
        second = jnp.where(keep, second, zero) + jnp.where(used & to_second, tile, zero)
        sums[0, t] = first.astype(BF16)
        sums[1, t] = second.astype(BF16)
        lasts = tuple(
            jnp.where(used & (src == cluster), t, last)
            for last, cluster in zip(lasts, clusters)
        )
        return first, second, src, lasts

    blank = jnp.zeros((tall, tall), F32)
    running = (blank, blank, jnp.int32(-1), tuple(jnp.int32(-1) for _ in clusters))
    pl.semaphore_wait(barrier, len(peers))

    mine = packed.at[levels, own_rows, :]
    feature_copies = {
        (k, crossing): remote(
            mine,
            packed.at[k, own_rows, :],
            (y_send if crossing else x_send).at[k],
            (y_recv if crossing else x_recv).at[k],
            near[k] if k < levels else 0,
            crossing,
        )
        for crossing in (True, False)
        for k in (across if crossing else range(levels))
    }
    feature_order = sorted(
        feature_copies,
        key=lambda c: -(reach(near[c[0]]) if c[0] < levels else 9) - 2 * c[1],
    )
    for c in feature_order:
        feature_copies[c].start()

    for i in range(parts):
        tile_loads[i].wait()
        running = lax.fori_loop(i * part_slots, (i + 1) * part_slots, one_tile, running)
    theirs = packed.at[levels, other_rows, :]
    relays = [
        remote(theirs, packed.at[k, other_rows, :], y_send.at[k], y_recv.at[k], near[k])
        for k in relayed
    ]
    if relayed:
        remote(
            mine, theirs, y_send.at[levels], y_recv.at[levels], near[0], True
        ).wait_recv()
    for copy in relays:
        copy.start()

    for j, last in enumerate(running[3]):
        at = jnp.maximum(last, 0)
        for d in range(2):
            block = sums[d, at]
            dense[j // 2, d * tall : (d + 1) * tall, (j % 2) * tall : (j % 2 + 1) * tall] = (
                jnp.where(last >= 0, block, jnp.zeros_like(block))
            )

    for load in loads[4:]:
        load.wait()
    turned[...] = weights[...].astype(F32).T.astype(BF16)
    gout_turned[...] = gouts[...].astype(F32).T
    bias_turned = jnp.broadcast_to(biases[...], (tall, biases.shape[1])).T

    by_lanes = (((1,), (1,)), ((), ()))
    total = None
    for k in [levels] + far_near[::-1]:
        if k < levels:
            feature_copies[k, False].wait_recv()
        if k < levels or not relayed:
            remote(
                mine, packed.at[k, other_rows, :], y_send.at[k], y_recv.at[k], near[0], True
            ).wait_recv()
        term = lax.dot_general(packed[k], dense[k], by_lanes, preferred_element_type=F32)
        total = term if total is None else total + term
    agg_all = total.astype(BF16)

    node_lane = lax.broadcasted_iota(jnp.int32, (turned.shape[0], nodes), 1)
    live_all = node_lane < jnp.where(node_lane < tall, size_ref[0], size_ref[1] + tall)
    pre = jnp.dot(turned[...], agg_all, preferred_element_type=F32)
    pre = pre + jnp.concatenate([bias_turned] * (nodes // tall), axis=1)
    gate = jax.nn.sigmoid(pre)
    hidden = jnp.where(live_all, pre * gate, 0.0)
    grad = gout_turned[...] * gate * (1.0 + pre * (1.0 - gate))
    grad = jnp.where(live_all, grad, 0.0).astype(BF16)

    ones = jnp.ones((16, nodes), BF16)
    grad_weight = lax.dot_general(
        jnp.concatenate([agg_all, ones], axis=0),
        grad,
        by_lanes,
        preferred_element_type=F32,
    )
    wide_feat, units = gw_ref.shape
    chunk = wide_feat // wide_count
    for j in range(wide_count):
        stage[j, :chunk] = grad_weight[j * chunk : (j + 1) * chunk]
        stage[j, chunk:] = grad_weight[wide_feat : wide_feat + 8]
    my_wide, my_deep = me.place(wide), me.place(deep)
    scatter_copies = []
    for m in far_wide:
        scatter_copies.append(
            remote(
                stage.at[me.place(wide, wide[m])],
                fold_in.at[my_wide],
                r1_send.at[m],
                r1_recv.at[m],
                wide[m],
            )
        )
        scatter_copies[-1].start()
    fold_in[my_wide] = stage[my_wide]

    part_back[...] = jnp.dot(weights[...], grad, preferred_element_type=F32)
    half_copy = remote(
        part_back.at[other_rows, :], part_in, p_send.at[0], p_recv.at[0], 0, True
    )
    half_copy.start()
    hidden_ref[...] = hidden.T.astype(BF16)

    for m in far_wide[::-1]:
        there = me.place(wide, wide[m])
        remote(
            stage.at[0], fold_in.at[there], r1_send.at[m], r1_recv.at[m], wide[m]
        ).wait_recv()
    part = fold_in[0]
    for m in range(1, wide_count):
        part = part + fold_in[m]
    fold_mid[my_deep] = part[:chunk].astype(fold_mid.dtype)
    bias_mid[my_deep] = part[chunk : chunk + 1]
    deep_copies = []
    for m in far_deep:
        for fold, send, recv in ((fold_mid, r2_send, r2_recv), (bias_mid, b2_send, b2_recv)):
            deep_copies.append(
                remote(fold.at[my_deep], fold.at[my_deep], send.at[m], recv.at[m], deep[m])
            )
            deep_copies[-1].start()

    half_copy.wait_recv()
    grad_agg = (part_back[own_rows, :] + part_in[...]).astype(BF16)
    back_copies = [
        remote(give.at[k], take.at[k], c_send.at[k], c_recv.at[k], near[k])
        for k in range(levels)
    ]
    for k in far_near[::-1]:
        give[k] = jnp.dot(grad_agg, dense[k], preferred_element_type=F32).astype(BF16)
        back_copies[k].start()
    own_back[...] = jnp.dot(grad_agg, dense[levels], preferred_element_type=F32)

    for m in far_deep[::-1]:
        there = me.place(deep, deep[m])
        for fold, send, recv in ((fold_mid, r2_send, r2_recv), (bias_mid, b2_send, b2_recv)):
            remote(
                fold.at[there], fold.at[there], send.at[m], recv.at[m], deep[m]
            ).wait_recv()
    part, bias_part = fold_mid[0].astype(F32), bias_mid[0]
    for m in range(1, deep_count):
        part, bias_part = part + fold_mid[m].astype(F32), bias_part + bias_mid[m]
    fold_all[my_wide] = part * scale
    gather_copies = [
        remote(
            fold_all.at[my_wide], fold_all.at[my_wide], r3_send.at[m], r3_recv.at[m], wide[m]
        )
        for m in far_wide
    ]
    for copy in gather_copies:
        copy.start()
    gb_ref[...] = bias_part * scale

    back = own_back[...]
    for k in far_near[::-1]:
        back_copies[k].wait_recv()
        back = back + take[k].astype(F32)
    gf_ref[...] = jnp.where(live, back, 0.0).astype(BF16)

    for m in far_wide[::-1]:
        remote(
            fold_all.at[my_wide],
            fold_all.at[me.place(wide, wide[m])],
            r3_send.at[m],
            r3_recv.at[m],
            wide[m],
        ).wait_recv()
    gw_ref[...] = fold_all[...].reshape(gw_ref.shape)

    for copy in (
        list(feature_copies.values())
        + relays
        + scatter_copies
        + [half_copy]
        + back_copies
        + deep_copies
        + gather_copies
    ):
        copy.wait_send()


def write_kernel(*refs):
    count = (len(refs) - 1) // 2
    sem = refs[-1]
    copies = [
        pltpu.make_async_copy(refs[i], refs[count + i], sem.at[i]) for i in range(count)
    ]
    for copy in copies:
        copy.start()
    for copy in copies:
        copy.wait()


def group_masks(bits):
    return [
        sum(1 << bit for place, bit in enumerate(bits) if m >> place & 1)
        for m in range(1 << len(bits))
    ]


def solution(mesh):
    row_groups = mesh.shape["rows"]
    levels = row_groups.bit_length() - 1
    wide_bits = [bit for bit in range(levels) if bit in (0, 4, 5)]
    deep_bits = [bit for bit in range(levels) if bit not in wide_bits]
    near = [1 << bit for bit in range(levels)]
    wide, deep = group_masks(wide_bits), group_masks(deep_bits)

    def local(
        features, adj_tiles, tile_src, tile_dst, tile_count, cluster_size, weight, bias, grad_out
    ):
        slots, tall, _ = adj_tiles.shape
        nodes, half = features.shape
        wide_feat, units = weight.shape
        chunk = wide_feat // len(wide)
        dma = pltpu.SemaphoreType.DMA
        plan = (near, wide, deep, 1.0 / math.sqrt(nodes * row_groups))
        shapes = [
            ((nodes, units), BF16),
            ((wide_feat, units), F32),
            ((1, units), F32),
            ((half, nodes), BF16),
        ]
        inputs = [
            tile_src,
            tile_dst,
            tile_count,
            cluster_size,
            features.T,
            adj_tiles,
            weight,
            bias.reshape(1, units),
            grad_out,
        ]
        results = pl.pallas_call(
            functools.partial(layer_kernel, plan),
            out_shape=tuple(pltpu.VMEM(shape, kind) for shape, kind in shapes),
            in_specs=[
                pl.BlockSpec(memory_space=pltpu.SMEM if x is tile_count else pltpu.HBM)
                for x in inputs
            ],
            out_specs=(pl.BlockSpec(memory_space=pltpu.VMEM),) * len(shapes),
            scratch_shapes=[
                pltpu.SMEM((slots,), jnp.int32),
                pltpu.SMEM((slots,), jnp.int32),
                pltpu.SMEM((2,), jnp.int32),
                pltpu.VMEM((half, nodes), BF16),
                pltpu.VMEM((slots, tall, tall), BF16),
                pltpu.VMEM((wide_feat, units), BF16),
                pltpu.VMEM((1, units), F32),
                pltpu.VMEM((nodes, units), BF16),
                pltpu.VMEM((levels + 1, wide_feat, nodes), BF16),
                pltpu.VMEM((2, slots, tall, tall), BF16),
                pltpu.VMEM((levels + 1, nodes, nodes), BF16),
                pltpu.VMEM((units, wide_feat), BF16),
                pltpu.VMEM((units, nodes), F32),
                pltpu.VMEM((wide_feat, nodes), F32),
                pltpu.VMEM((half, nodes), F32),
                pltpu.VMEM((len(wide), chunk + 8, units), F32),
                pltpu.VMEM((len(wide), chunk + 8, units), F32),
                pltpu.VMEM((len(deep), chunk, units), MID),
                pltpu.VMEM((len(wide), chunk, units), F32),
                pltpu.VMEM((len(deep), 1, units), F32),
                pltpu.VMEM((levels, half, nodes), BF16),
                pltpu.VMEM((levels, half, nodes), BF16),
                pltpu.VMEM((half, nodes), F32),
                dma((7,)),
                dma((PARTS,)),
                dma((levels,)),
                dma((levels,)),
                dma((levels + 1,)),
                dma((levels + 1,)),
                dma((1,)),
                dma((1,)),
                dma((levels,)),
                dma((levels,)),
                dma((len(wide),)),
                dma((len(wide),)),
                dma((len(deep),)),
                dma((len(deep),)),
                dma((len(wide),)),
                dma((len(wide),)),
                dma((len(deep),)),
                dma((len(deep),)),
            ],
            compiler_params=pltpu.CompilerParams(
                collective_id=0, has_side_effects=True, vmem_limit_bytes=40 * 1024 * 1024
            ),
            name="graph_layer",
        )(
            *[
                x if x is tile_count else pltpu.with_memory_space_constraint(x, pltpu.HBM)
                for x in inputs
            ]
        )
        hidden, grad_weight, grad_bias, grad_features = pl.pallas_call(
            write_kernel,
            out_shape=tuple(pltpu.HBM(shape, kind) for shape, kind in shapes),
            in_specs=[pl.BlockSpec(memory_space=pltpu.VMEM)] * len(shapes),
            out_specs=(pl.BlockSpec(memory_space=pltpu.HBM),) * len(shapes),
            scratch_shapes=[dma((len(shapes),))],
            name="write_results",
        )(*[pltpu.with_memory_space_constraint(x, pltpu.VMEM) for x in results])
        return hidden, grad_weight, grad_bias.reshape(units), grad_features.T

    return jax.shard_map(
        local,
        mesh=mesh,
        in_specs=(
            P("rows", "cols"),
            P("rows", None, None),
            P("rows"),
            P("rows"),
            P("rows"),
            P("rows"),
            P(None, "cols"),
            P("cols"),
            P("rows", "cols"),
        ),
        out_specs=(P("rows", "cols"), P(None, "cols"), P("cols"), P("rows", "cols")),
        check_vma=False,
    )
```

```python
import functools
import math

import jax
import jax.numpy as jnp
from jax import lax
from jax.experimental import pallas as pl
from jax.experimental.pallas import tpu as pltpu
from jax.sharding import PartitionSpec as P

F32 = jnp.float32
BF16 = jnp.bfloat16
MESH = pl.DeviceIdType.MESH
PARTS = 4
MID = jnp.bfloat16
RELAY = (1, 16)


class Spot:
    def __init__(self, index, levels):
        self.index = index
        self.levels = levels
        self.bits = [lax.rem(lax.div(index, jnp.int32(1 << b)), jnp.int32(2)) for b in range(levels)]

    def flipped(self, mask):
        out = self.index
        for b in range(self.levels):
            if mask >> b & 1:
                out = out + ((1 << b) - (2 << b) * self.bits[b])
        return out

    def place(self, masks, mask=0):
        out = jnp.int32(0)
        for p in range(len(masks).bit_length() - 1):
            bit = self.bits[masks[1 << p].bit_length() - 1]
            out = out + (1 << p) * (1 - bit if masks[1 << p] & mask else bit)
        return out


def reach(mask):
    z, y, x = mask >> 1 & 7, mask >> 4 & 3, mask >> 6
    far_z = max(min(abs((a ^ z) - a), 8 - abs((a ^ z) - a)) for a in range(8))
    far_y = max(min(abs((a ^ y) - a), 4 - abs((a ^ y) - a)) for a in range(4))
    return far_z + far_y + x


def layer_kernel(
    plan,
    src_hbm,
    dst_hbm,
    count_ref,
    size_hbm,
    feat_hbm,
    tiles_hbm,
    weight_hbm,
    bias_hbm,
    gout_hbm,
    hidden_ref,
    gw_ref,
    gb_ref,
    gf_ref,
    src_ref,
    dst_ref,
    size_ref,
    feat,
    tiles,
    weights,
    biases,
    gouts,
    packed,
    sums,
    dense,
    turned,
    gout_turned,
    part_back,
    part_in,
    stage,
    fold_in,
    fold_mid,
    fold_all,
    bias_mid,
    give,
    take,
    own_back,
    load_sem,
    tile_sem,
    x_send,
    x_recv,
    y_send,
    y_recv,
    p_send,
    p_recv,
    c_send,
    c_recv,
    r1_send,
    r1_recv,
    r2_send,
    r2_recv,
    r3_send,
    r3_recv,
    b2_send,
    b2_recv,
):
    near, wide, deep, scale = plan
    levels = len(near)
    wide_count, deep_count = len(wide), len(deep)
    me = Spot(lax.axis_index("rows"), levels)
    col = lax.axis_index("cols")
    slots, tall, _ = tiles.shape
    half, nodes = feat.shape
    own_rows = pl.ds(pl.multiple_of(col * half, half), half)
    other_rows = pl.ds(pl.multiple_of((1 - col) * half, half), half)
    relayed = [k for k in range(levels) if near[k] in RELAY]
    across = [k for k in range(levels + 1) if k not in relayed]
    far_near = sorted(range(levels), key=lambda k: -reach(near[k]))
    far_wide = sorted(range(1, wide_count), key=lambda m: -reach(wide[m]))
    far_deep = sorted(range(1, deep_count), key=lambda m: (-(deep[m] & 8), -reach(deep[m])))
    parts = tile_sem.shape[0]
    part_slots = slots // parts

    def remote(src, dst, send, recv, mask, crossing=False):
        who = {"rows": me.flipped(mask)} if mask else {}
        if crossing:
            who["cols"] = 1 - col
        return pltpu.make_async_remote_copy(
            src_ref=src,
            dst_ref=dst,
            send_sem=send,
            recv_sem=recv,
            device_id=who,
            device_id_type=MESH,
        )

    peers = [(mask, False) for mask in set(near) | set(wide[1:]) | set(deep[1:])]
    peers += [(near[k] if k < levels else 0, True) for k in across]
    peers.sort(key=lambda peer: -reach(peer[0]) - 2 * peer[1])
    barrier = pltpu.get_barrier_semaphore()
    for mask, crossing in peers:
        who = {"rows": me.flipped(mask)} if mask else {}
        if crossing:
            who["cols"] = 1 - col
        pl.semaphore_signal(barrier, inc=1, device_id=who, device_id_type=MESH)

    loads = [
        pltpu.make_async_copy(here, there, load_sem.at[i])
        for i, (here, there) in enumerate(
            [
                (size_hbm, size_ref),
                (feat_hbm, feat),
                (src_hbm, src_ref),
                (dst_hbm, dst_ref),
                (weight_hbm, weights),
                (bias_hbm, biases),
                (gout_hbm, gouts),
            ]
        )
    ]
    tile_loads = [
        pltpu.make_async_copy(
            tiles_hbm.at[pl.ds(i * part_slots, part_slots)],
            tiles.at[pl.ds(i * part_slots, part_slots)],
            tile_sem.at[i],
        )
        for i in range(parts)
    ]
    for load in loads + tile_loads:
        load.start()

    loads[0].wait()
    loads[1].wait()
    node_lane = lax.broadcasted_iota(jnp.int32, (half, nodes), 1)
    live = node_lane < jnp.where(node_lane < tall, size_ref[0], size_ref[1] + tall)
    packed[levels, own_rows, :] = jnp.where(live, feat[...].astype(F32), 0.0).astype(BF16)

    clusters = []
    for k in range(levels + 1):
        group = me.flipped(near[k]) if k < levels else me.index
        clusters += [group * 2, group * 2 + 1]
    for load in loads[2:4]:
        load.wait()
    count = count_ref[0]

    def one_tile(t, carried):
        first, second, prev, lasts = carried
        src = src_ref[t]
        used = t < count
        keep = (src == prev) & used
        to_second = dst_ref[t] == 1
        tile = tiles[t].astype(F32)
        zero = jnp.zeros_like(tile)
        first = jnp.where(keep, first, zero) + jnp.where(used & (~to_second), tile, zero)
        second = jnp.where(keep, second, zero) + jnp.where(used & to_second, tile, zero)
        sums[0, t] = first.astype(BF16)
        sums[1, t] = second.astype(BF16)
        lasts = tuple(
            jnp.where(used & (src == cluster), t, last)
            for last, cluster in zip(lasts, clusters)
        )
        return first, second, src, lasts

    blank = jnp.zeros((tall, tall), F32)
    running = (blank, blank, jnp.int32(-1), tuple(jnp.int32(-1) for _ in clusters))
    pl.semaphore_wait(barrier, len(peers))

    mine = packed.at[levels, own_rows, :]
    feature_copies = {
        (k, crossing): remote(
            mine,
            packed.at[k, own_rows, :],
            (y_send if crossing else x_send).at[k],
            (y_recv if crossing else x_recv).at[k],
            near[k] if k < levels else 0,
            crossing,
        )
        for crossing in (True, False)
        for k in (across if crossing else range(levels))
    }
    feature_order = sorted(
        feature_copies,
        key=lambda c: -(reach(near[c[0]]) if c[0] < levels else 9) - 2 * c[1],
    )
    for c in feature_order:
        feature_copies[c].start()

    for i in range(parts):
        tile_loads[i].wait()
        running = lax.fori_loop(i * part_slots, (i + 1) * part_slots, one_tile, running)
    theirs = packed.at[levels, other_rows, :]
    relays = [
        remote(theirs, packed.at[k, other_rows, :], y_send.at[k], y_recv.at[k], near[k])
        for k in relayed
    ]
    if relayed:
        remote(
            mine, theirs, y_send.at[levels], y_recv.at[levels], near[0], True
        ).wait_recv()
    for copy in relays:
        copy.start()

    for j, last in enumerate(running[3]):
        at = jnp.maximum(last, 0)
        for d in range(2):
            block = sums[d, at]
            dense[j // 2, d * tall : (d + 1) * tall, (j % 2) * tall : (j % 2 + 1) * tall] = (
                jnp.where(last >= 0, block, jnp.zeros_like(block))
            )

    for load in loads[4:]:
        load.wait()
    turned[...] = weights[...].astype(F32).T.astype(BF16)
    gout_turned[...] = gouts[...].astype(F32).T
    bias_turned = jnp.broadcast_to(biases[...], (tall, biases.shape[1])).T

    by_lanes = (((1,), (1,)), ((), ()))
    total = None
    for k in [levels] + far_near[::-1]:
        if k < levels:
            feature_copies[k, False].wait_recv()
        if k < levels or not relayed:
            remote(
                mine, packed.at[k, other_rows, :], y_send.at[k], y_recv.at[k], near[0], True
            ).wait_recv()
        term = lax.dot_general(packed[k], dense[k], by_lanes, preferred_element_type=F32)
        total = term if total is None else total + term
    agg_all = total.astype(BF16)

    node_lane = lax.broadcasted_iota(jnp.int32, (turned.shape[0], nodes), 1)
    live_all = node_lane < jnp.where(node_lane < tall, size_ref[0], size_ref[1] + tall)
    pre = jnp.dot(turned[...], agg_all, preferred_element_type=F32)
    pre = pre + jnp.concatenate([bias_turned] * (nodes // tall), axis=1)
    gate = jax.nn.sigmoid(pre)
    hidden = jnp.where(live_all, pre * gate, 0.0)
    grad = gout_turned[...] * gate * (1.0 + pre * (1.0 - gate))
    grad = jnp.where(live_all, grad, 0.0).astype(BF16)

    ones = jnp.ones((16, nodes), BF16)
    grad_weight = lax.dot_general(
        jnp.concatenate([agg_all, ones], axis=0),
        grad,
        by_lanes,
        preferred_element_type=F32,
    )
    wide_feat, units = gw_ref.shape
    chunk = wide_feat // wide_count
    for j in range(wide_count):
        stage[j, :chunk] = grad_weight[j * chunk : (j + 1) * chunk]
        stage[j, chunk:] = grad_weight[wide_feat : wide_feat + 8]
    my_wide, my_deep = me.place(wide), me.place(deep)
    scatter_copies = []
    for m in far_wide:
        scatter_copies.append(
            remote(
                stage.at[me.place(wide, wide[m])],
                fold_in.at[my_wide],
                r1_send.at[m],
                r1_recv.at[m],
                wide[m],
            )
        )
        scatter_copies[-1].start()
    fold_in[my_wide] = stage[my_wide]

    part_back[...] = jnp.dot(weights[...], grad, preferred_element_type=F32)
    half_copy = remote(
        part_back.at[other_rows, :], part_in, p_send.at[0], p_recv.at[0], 0, True
    )
    half_copy.start()
    hidden_ref[...] = hidden.T.astype(BF16)

    for m in far_wide[::-1]:
        there = me.place(wide, wide[m])
        remote(
            stage.at[0], fold_in.at[there], r1_send.at[m], r1_recv.at[m], wide[m]
        ).wait_recv()
    part = fold_in[0]
    for m in range(1, wide_count):
        part = part + fold_in[m]
    fold_mid[my_deep] = part[:chunk].astype(fold_mid.dtype)
    bias_mid[my_deep] = part[chunk : chunk + 1]
    deep_copies = []
    for m in far_deep:
        for fold, send, recv in ((fold_mid, r2_send, r2_recv), (bias_mid, b2_send, b2_recv)):
            deep_copies.append(
                remote(fold.at[my_deep], fold.at[my_deep], send.at[m], recv.at[m], deep[m])
            )
            deep_copies[-1].start()

    half_copy.wait_recv()
    grad_agg = (part_back[own_rows, :] + part_in[...]).astype(BF16)
    back_copies = [
        remote(give.at[k], take.at[k], c_send.at[k], c_recv.at[k], near[k])
        for k in range(levels)
    ]
    for k in far_near[::-1]:
        give[k] = jnp.dot(grad_agg, dense[k], preferred_element_type=F32).astype(BF16)
        back_copies[k].start()
    own_back[...] = jnp.dot(grad_agg, dense[levels], preferred_element_type=F32)

    for m in far_deep[::-1]:
        there = me.place(deep, deep[m])
        for fold, send, recv in ((fold_mid, r2_send, r2_recv), (bias_mid, b2_send, b2_recv)):
            remote(
                fold.at[there], fold.at[there], send.at[m], recv.at[m], deep[m]
            ).wait_recv()
    part, bias_part = fold_mid[0].astype(F32), bias_mid[0]
    for m in range(1, deep_count):
        part, bias_part = part + fold_mid[m].astype(F32), bias_part + bias_mid[m]
    fold_all[my_wide] = part * scale
    gather_copies = [
        remote(
            fold_all.at[my_wide], fold_all.at[my_wide], r3_send.at[m], r3_recv.at[m], wide[m]
        )
        for m in far_wide
    ]
    for copy in gather_copies:
        copy.start()
    gb_ref[...] = bias_part * scale

    back = own_back[...]
    for k in far_near[::-1]:
        back_copies[k].wait_recv()
        back = back + take[k].astype(F32)
    gf_ref[...] = jnp.where(live, back, 0.0).astype(BF16)

    for m in far_wide[::-1]:
        remote(
            fold_all.at[my_wide],
            fold_all.at[me.place(wide, wide[m])],
            r3_send.at[m],
            r3_recv.at[m],
            wide[m],
        ).wait_recv()
    gw_ref[...] = fold_all[...].reshape(gw_ref.shape)

    for copy in (
        list(feature_copies.values())
        + relays
        + scatter_copies
        + [half_copy]
        + back_copies
        + deep_copies
        + gather_copies
    ):
        copy.wait_send()


def write_kernel(*refs):
    count = (len(refs) - 1) // 2
    sem = refs[-1]
    copies = [
        pltpu.make_async_copy(refs[i], refs[count + i], sem.at[i]) for i in range(count)
    ]
    for copy in copies:
        copy.start()
    for copy in copies:
        copy.wait()


def group_masks(bits):
    return [
        sum(1 << bit for place, bit in enumerate(bits) if m >> place & 1)
        for m in range(1 << len(bits))
    ]


def solution(mesh):
    row_groups = mesh.shape["rows"]
    levels = row_groups.bit_length() - 1
    wide_bits = [bit for bit in range(levels) if bit in (0, 4, 5)]
    deep_bits = [bit for bit in range(levels) if bit not in wide_bits]
    near = [1 << bit for bit in range(levels)]
    wide, deep = group_masks(wide_bits), group_masks(deep_bits)

    def local(
        features, adj_tiles, tile_src, tile_dst, tile_count, cluster_size, weight, bias, grad_out
    ):
        slots, tall, _ = adj_tiles.shape
        nodes, half = features.shape
        wide_feat, units = weight.shape
        chunk = wide_feat // len(wide)
        dma = pltpu.SemaphoreType.DMA
        plan = (near, wide, deep, 1.0 / math.sqrt(nodes * row_groups))
        shapes = [
            ((nodes, units), BF16),
            ((wide_feat, units), F32),
            ((1, units), F32),
            ((half, nodes), BF16),
        ]
        inputs = [
            tile_src,
            tile_dst,
            tile_count,
            cluster_size,
            features.T,
            adj_tiles,
            weight,
            bias.reshape(1, units),
            grad_out,
        ]
        results = pl.pallas_call(
            functools.partial(layer_kernel, plan),
            out_shape=tuple(pltpu.VMEM(shape, kind) for shape, kind in shapes),
            in_specs=[
                pl.BlockSpec(memory_space=pltpu.SMEM if x is tile_count else pltpu.HBM)
                for x in inputs
            ],
            out_specs=(pl.BlockSpec(memory_space=pltpu.VMEM),) * len(shapes),
            scratch_shapes=[
                pltpu.SMEM((slots,), jnp.int32),
                pltpu.SMEM((slots,), jnp.int32),
                pltpu.SMEM((2,), jnp.int32),
                pltpu.VMEM((half, nodes), BF16),
                pltpu.VMEM((slots, tall, tall), BF16),
                pltpu.VMEM((wide_feat, units), BF16),
                pltpu.VMEM((1, units), F32),
                pltpu.VMEM((nodes, units), BF16),
                pltpu.VMEM((levels + 1, wide_feat, nodes), BF16),
                pltpu.VMEM((2, slots, tall, tall), BF16),
                pltpu.VMEM((levels + 1, nodes, nodes), BF16),
                pltpu.VMEM((units, wide_feat), BF16),
                pltpu.VMEM((units, nodes), F32),
                pltpu.VMEM((wide_feat, nodes), F32),
                pltpu.VMEM((half, nodes), F32),
                pltpu.VMEM((len(wide), chunk + 8, units), F32),
                pltpu.VMEM((len(wide), chunk + 8, units), F32),
                pltpu.VMEM((len(deep), chunk, units), MID),
                pltpu.VMEM((len(wide), chunk, units), F32),
                pltpu.VMEM((len(deep), 1, units), F32),
                pltpu.VMEM((levels, half, nodes), BF16),
                pltpu.VMEM((levels, half, nodes), BF16),
                pltpu.VMEM((half, nodes), F32),
                dma((7,)),
                dma((PARTS,)),
                dma((levels,)),
                dma((levels,)),
                dma((levels + 1,)),
                dma((levels + 1,)),
                dma((1,)),
                dma((1,)),
                dma((levels,)),
                dma((levels,)),
                dma((len(wide),)),
                dma((len(wide),)),
                dma((len(deep),)),
                dma((len(deep),)),
                dma((len(wide),)),
                dma((len(wide),)),
                dma((len(deep),)),
                dma((len(deep),)),
            ],
            compiler_params=pltpu.CompilerParams(
                collective_id=0, has_side_effects=True, vmem_limit_bytes=40 * 1024 * 1024
            ),
            name="graph_layer",
        )(
            *[
                x if x is tile_count else pltpu.with_memory_space_constraint(x, pltpu.HBM)
                for x in inputs
            ]
        )
        hidden, grad_weight, grad_bias, grad_features = pl.pallas_call(
            write_kernel,
            out_shape=tuple(pltpu.HBM(shape, kind) for shape, kind in shapes),
            in_specs=[pl.BlockSpec(memory_space=pltpu.VMEM)] * len(shapes),
            out_specs=(pl.BlockSpec(memory_space=pltpu.HBM),) * len(shapes),
            scratch_shapes=[dma((len(shapes),))],
            name="write_results",
        )(*[pltpu.with_memory_space_constraint(x, pltpu.VMEM) for x in results])
        return hidden, grad_weight, grad_bias.reshape(units), grad_features.T

    return jax.shard_map(
        local,
        mesh=mesh,
        in_specs=(
            P("rows", "cols"),
            P("rows", None, None),
            P("rows"),
            P("rows"),
            P("rows"),
            P("rows"),
            P(None, "cols"),
            P("cols"),
            P("rows", "cols"),
        ),
        out_specs=(P("rows", "cols"), P(None, "cols"), P("cols"), P("rows", "cols")),
        check_vma=False,
    )
```

```python
import functools
import math

import jax
import jax.numpy as jnp
from jax import lax
from jax.experimental import pallas as pl
from jax.experimental.pallas import tpu as pltpu
from jax.sharding import PartitionSpec as P

F32 = jnp.float32
BF16 = jnp.bfloat16
MESH = pl.DeviceIdType.MESH
PARTS = 4
MID = jnp.bfloat16
RELAY = 0


class Spot:
    def __init__(self, index, levels):
        self.index = index
        self.levels = levels
        self.bits = [lax.rem(lax.div(index, jnp.int32(1 << b)), jnp.int32(2)) for b in range(levels)]

    def flipped(self, mask):
        out = self.index
        for b in range(self.levels):
            if mask >> b & 1:
                out = out + ((1 << b) - (2 << b) * self.bits[b])
        return out

    def place(self, masks, mask=0):
        out = jnp.int32(0)
        for p in range(len(masks).bit_length() - 1):
            bit = self.bits[masks[1 << p].bit_length() - 1]
            out = out + (1 << p) * (1 - bit if masks[1 << p] & mask else bit)
        return out


def reach(mask):
    z, y, x = mask >> 1 & 7, mask >> 4 & 3, mask >> 6
    far_z = max(min(abs((a ^ z) - a), 8 - abs((a ^ z) - a)) for a in range(8))
    far_y = max(min(abs((a ^ y) - a), 4 - abs((a ^ y) - a)) for a in range(4))
    return far_z + far_y + x


def layer_kernel(
    plan,
    src_hbm,
    dst_hbm,
    count_ref,
    size_hbm,
    feat_hbm,
    tiles_hbm,
    weight_hbm,
    bias_hbm,
    gout_hbm,
    hidden_ref,
    gw_ref,
    gb_ref,
    gf_ref,
    src_ref,
    dst_ref,
    size_ref,
    feat,
    tiles,
    weights,
    biases,
    gouts,
    packed,
    sums,
    dense,
    turned,
    gout_turned,
    part_back,
    part_in,
    stage,
    fold_in,
    fold_mid,
    fold_all,
    bias_mid,
    give,
    take,
    own_back,
    load_sem,
    tile_sem,
    x_send,
    x_recv,
    y_send,
    y_recv,
    p_send,
    p_recv,
    c_send,
    c_recv,
    r1_send,
    r1_recv,
    r2_send,
    r2_recv,
    r3_send,
    r3_recv,
    b2_send,
    b2_recv,
):
    near, wide, deep, scale = plan
    levels = len(near)
    wide_count, deep_count = len(wide), len(deep)
    me = Spot(lax.axis_index("rows"), levels)
    col = lax.axis_index("cols")
    slots, tall, _ = tiles.shape
    half, nodes = feat.shape
    own_rows = pl.ds(pl.multiple_of(col * half, half), half)
    other_rows = pl.ds(pl.multiple_of((1 - col) * half, half), half)
    relayed = [k for k in range(levels) if reach(near[k]) <= RELAY]
    across = [k for k in range(levels + 1) if k not in relayed]
    far_near = sorted(range(levels), key=lambda k: -reach(near[k]))
    far_wide = sorted(range(1, wide_count), key=lambda m: -reach(wide[m]))
    far_deep = sorted(range(1, deep_count), key=lambda m: (-(deep[m] & 8), -reach(deep[m])))
    parts = tile_sem.shape[0]
    part_slots = slots // parts

    def remote(src, dst, send, recv, mask, crossing=False):
        who = {"rows": me.flipped(mask)} if mask else {}
        if crossing:
            who["cols"] = 1 - col
        return pltpu.make_async_remote_copy(
            src_ref=src,
            dst_ref=dst,
            send_sem=send,
            recv_sem=recv,
            device_id=who,
            device_id_type=MESH,
        )

    peers = [(mask, False) for mask in set(near) | set(wide[1:]) | set(deep[1:])]
    peers += [(near[k] if k < levels else 0, True) for k in across]
    peers.sort(key=lambda peer: -reach(peer[0]) - 2 * peer[1])
    barrier = pltpu.get_barrier_semaphore()
    for mask, crossing in peers:
        who = {"rows": me.flipped(mask)} if mask else {}
        if crossing:
            who["cols"] = 1 - col
        pl.semaphore_signal(barrier, inc=1, device_id=who, device_id_type=MESH)

    loads = [
        pltpu.make_async_copy(here, there, load_sem.at[i])
        for i, (here, there) in enumerate(
            [
                (size_hbm, size_ref),
                (feat_hbm, feat),
                (src_hbm, src_ref),
                (dst_hbm, dst_ref),
                (weight_hbm, weights),
                (bias_hbm, biases),
                (gout_hbm, gouts),
            ]
        )
    ]
    tile_loads = [
        pltpu.make_async_copy(
            tiles_hbm.at[pl.ds(i * part_slots, part_slots)],
            tiles.at[pl.ds(i * part_slots, part_slots)],
            tile_sem.at[i],
        )
        for i in range(parts)
    ]
    for load in loads + tile_loads:
        load.start()

    loads[0].wait()
    loads[1].wait()
    node_lane = lax.broadcasted_iota(jnp.int32, (half, nodes), 1)
    live = node_lane < jnp.where(node_lane < tall, size_ref[0], size_ref[1] + tall)
    packed[levels, own_rows, :] = jnp.where(live, feat[...].astype(F32), 0.0).astype(BF16)

    clusters = []
    for k in range(levels + 1):
        group = me.flipped(near[k]) if k < levels else me.index
        clusters += [group * 2, group * 2 + 1]
    for load in loads[2:4]:
        load.wait()
    count = count_ref[0]

    def one_tile(t, carried):
        first, second, prev, lasts = carried
        src = src_ref[t]
        used = t < count
        keep = (src == prev) & used
        to_second = dst_ref[t] == 1
        tile = tiles[t].astype(F32)
        zero = jnp.zeros_like(tile)
        first = jnp.where(keep, first, zero) + jnp.where(used & (~to_second), tile, zero)
        second = jnp.where(keep, second, zero) + jnp.where(used & to_second, tile, zero)
        sums[0, t] = first.astype(BF16)
        sums[1, t] = second.astype(BF16)
        lasts = tuple(
            jnp.where(used & (src == cluster), t, last)
            for last, cluster in zip(lasts, clusters)
        )
        return first, second, src, lasts

    blank = jnp.zeros((tall, tall), F32)
    running = (blank, blank, jnp.int32(-1), tuple(jnp.int32(-1) for _ in clusters))
    pl.semaphore_wait(barrier, len(peers))

    mine = packed.at[levels, own_rows, :]
    feature_copies = {
        (k, crossing): remote(
            mine,
            packed.at[k, own_rows, :],
            (y_send if crossing else x_send).at[k],
            (y_recv if crossing else x_recv).at[k],
            near[k] if k < levels else 0,
            crossing,
        )
        for crossing in (True, False)
        for k in (across if crossing else range(levels))
    }
    feature_order = sorted(
        feature_copies,
        key=lambda c: -(reach(near[c[0]]) if c[0] < levels else 9) - 2 * c[1],
    )
    for c in feature_order:
        feature_copies[c].start()

    for i in range(parts):
        tile_loads[i].wait()
        running = lax.fori_loop(i * part_slots, (i + 1) * part_slots, one_tile, running)
    theirs = packed.at[levels, other_rows, :]
    relays = [
        remote(theirs, packed.at[k, other_rows, :], y_send.at[k], y_recv.at[k], near[k])
        for k in relayed
    ]
    if relayed:
        remote(
            mine, theirs, y_send.at[levels], y_recv.at[levels], near[0], True
        ).wait_recv()
    for copy in relays:
        copy.start()

    for j, last in enumerate(running[3]):
        at = jnp.maximum(last, 0)
        for d in range(2):
            block = sums[d, at]
            dense[j // 2, d * tall : (d + 1) * tall, (j % 2) * tall : (j % 2 + 1) * tall] = (
                jnp.where(last >= 0, block, jnp.zeros_like(block))
            )

    for load in loads[4:]:
        load.wait()
    turned[...] = weights[...].astype(F32).T.astype(BF16)
    gout_turned[...] = gouts[...].astype(F32).T
    bias_turned = jnp.broadcast_to(biases[...], (tall, biases.shape[1])).T

    by_lanes = (((1,), (1,)), ((), ()))
    total = None
    for k in [levels] + far_near[::-1]:
        if k < levels:
            feature_copies[k, False].wait_recv()
        if k < levels or not relayed:
            remote(
                mine, packed.at[k, other_rows, :], y_send.at[k], y_recv.at[k], near[0], True
            ).wait_recv()
        term = lax.dot_general(packed[k], dense[k], by_lanes, preferred_element_type=F32)
        total = term if total is None else total + term
    agg_all = total.astype(BF16)

    node_lane = lax.broadcasted_iota(jnp.int32, (turned.shape[0], nodes), 1)
    live_all = node_lane < jnp.where(node_lane < tall, size_ref[0], size_ref[1] + tall)
    pre = jnp.dot(turned[...], agg_all, preferred_element_type=F32)
    pre = pre + jnp.concatenate([bias_turned] * (nodes // tall), axis=1)
    gate = jax.nn.sigmoid(pre)
    hidden = jnp.where(live_all, pre * gate, 0.0)
    grad = gout_turned[...] * gate * (1.0 + pre * (1.0 - gate))
    grad = jnp.where(live_all, grad, 0.0).astype(BF16)

    ones = jnp.ones((16, nodes), BF16)
    grad_weight = lax.dot_general(
        jnp.concatenate([agg_all, ones], axis=0),
        grad,
        by_lanes,
        preferred_element_type=F32,
    )
    wide_feat, units = gw_ref.shape
    chunk = wide_feat // wide_count
    for j in range(wide_count):
        stage[j, :chunk] = grad_weight[j * chunk : (j + 1) * chunk]
        stage[j, chunk:] = grad_weight[wide_feat : wide_feat + 8]
    my_wide, my_deep = me.place(wide), me.place(deep)
    scatter_copies = []
    for m in far_wide:
        scatter_copies.append(
            remote(
                stage.at[me.place(wide, wide[m])],
                fold_in.at[my_wide],
                r1_send.at[m],
                r1_recv.at[m],
                wide[m],
            )
        )
        scatter_copies[-1].start()
    fold_in[my_wide] = stage[my_wide]

    part_back[...] = jnp.dot(weights[...], grad, preferred_element_type=F32)
    half_copy = remote(
        part_back.at[other_rows, :], part_in, p_send.at[0], p_recv.at[0], 0, True
    )
    half_copy.start()
    hidden_ref[...] = hidden.T.astype(BF16)

    for m in far_wide[::-1]:
        there = me.place(wide, wide[m])
        remote(
            stage.at[0], fold_in.at[there], r1_send.at[m], r1_recv.at[m], wide[m]
        ).wait_recv()
    part = fold_in[0]
    for m in range(1, wide_count):
        part = part + fold_in[m]
    fold_mid[my_deep] = part[:chunk].astype(fold_mid.dtype)
    bias_mid[my_deep] = part[chunk : chunk + 1]
    deep_copies = []
    first = len(far_deep) // 4
    for fold, send, recv, which in (
        (fold_mid, r2_send, r2_recv, far_deep[:first]),
        (bias_mid, b2_send, b2_recv, far_deep[:first]),
        (fold_mid, r2_send, r2_recv, far_deep[first:]),
        (bias_mid, b2_send, b2_recv, far_deep[first:]),
    ):
        for m in which:
            deep_copies.append(
                remote(fold.at[my_deep], fold.at[my_deep], send.at[m], recv.at[m], deep[m])
            )
            deep_copies[-1].start()

    half_copy.wait_recv()
    grad_agg = (part_back[own_rows, :] + part_in[...]).astype(BF16)
    back_copies = [
        remote(give.at[k], take.at[k], c_send.at[k], c_recv.at[k], near[k])
        for k in range(levels)
    ]
    for k in far_near[::-1]:
        give[k] = jnp.dot(grad_agg, dense[k], preferred_element_type=F32).astype(BF16)
        back_copies[k].start()
    own_back[...] = jnp.dot(grad_agg, dense[levels], preferred_element_type=F32)

    for m in far_deep[::-1]:
        there = me.place(deep, deep[m])
        for fold, send, recv in ((fold_mid, r2_send, r2_recv), (bias_mid, b2_send, b2_recv)):
            remote(
                fold.at[there], fold.at[there], send.at[m], recv.at[m], deep[m]
            ).wait_recv()
    part, bias_part = fold_mid[0].astype(F32), bias_mid[0]
    for m in range(1, deep_count):
        part, bias_part = part + fold_mid[m].astype(F32), bias_part + bias_mid[m]
    fold_all[my_wide] = part * scale
    gather_copies = [
        remote(
            fold_all.at[my_wide], fold_all.at[my_wide], r3_send.at[m], r3_recv.at[m], wide[m]
        )
        for m in far_wide
    ]
    for copy in gather_copies:
        copy.start()
    gb_ref[...] = bias_part * scale

    back = own_back[...]
    for k in far_near[::-1]:
        back_copies[k].wait_recv()
        back = back + take[k].astype(F32)
    gf_ref[...] = jnp.where(live, back, 0.0).astype(BF16)

    for m in far_wide[::-1]:
        remote(
            fold_all.at[my_wide],
            fold_all.at[me.place(wide, wide[m])],
            r3_send.at[m],
            r3_recv.at[m],
            wide[m],
        ).wait_recv()
    gw_ref[...] = fold_all[...].reshape(gw_ref.shape)

    for copy in (
        list(feature_copies.values())
        + relays
        + scatter_copies
        + [half_copy]
        + back_copies
        + deep_copies
        + gather_copies
    ):
        copy.wait_send()


def write_kernel(*refs):
    count = (len(refs) - 1) // 2
    sem = refs[-1]
    copies = [
        pltpu.make_async_copy(refs[i], refs[count + i], sem.at[i]) for i in range(count)
    ]
    for copy in copies:
        copy.start()
    for copy in copies:
        copy.wait()


def group_masks(bits):
    return [
        sum(1 << bit for place, bit in enumerate(bits) if m >> place & 1)
        for m in range(1 << len(bits))
    ]


def solution(mesh):
    row_groups = mesh.shape["rows"]
    levels = row_groups.bit_length() - 1
    wide_bits = [bit for bit in range(levels) if bit in (0, 4, 5)]
    deep_bits = [bit for bit in range(levels) if bit not in wide_bits]
    near = [1 << bit for bit in range(levels)]
    wide, deep = group_masks(wide_bits), group_masks(deep_bits)

    def local(
        features, adj_tiles, tile_src, tile_dst, tile_count, cluster_size, weight, bias, grad_out
    ):
        slots, tall, _ = adj_tiles.shape
        nodes, half = features.shape
        wide_feat, units = weight.shape
        chunk = wide_feat // len(wide)
        dma = pltpu.SemaphoreType.DMA
        plan = (near, wide, deep, 1.0 / math.sqrt(nodes * row_groups))
        shapes = [
            ((nodes, units), BF16),
            ((wide_feat, units), F32),
            ((1, units), F32),
            ((half, nodes), BF16),
        ]
        inputs = [
            tile_src,
            tile_dst,
            tile_count,
            cluster_size,
            features.T,
            adj_tiles,
            weight,
            bias.reshape(1, units),
            grad_out,
        ]
        results = pl.pallas_call(
            functools.partial(layer_kernel, plan),
            out_shape=tuple(pltpu.VMEM(shape, kind) for shape, kind in shapes),
            in_specs=[
                pl.BlockSpec(memory_space=pltpu.SMEM if x is tile_count else pltpu.HBM)
                for x in inputs
            ],
            out_specs=(pl.BlockSpec(memory_space=pltpu.VMEM),) * len(shapes),
            scratch_shapes=[
                pltpu.SMEM((slots,), jnp.int32),
                pltpu.SMEM((slots,), jnp.int32),
                pltpu.SMEM((2,), jnp.int32),
                pltpu.VMEM((half, nodes), BF16),
                pltpu.VMEM((slots, tall, tall), BF16),
                pltpu.VMEM((wide_feat, units), BF16),
                pltpu.VMEM((1, units), F32),
                pltpu.VMEM((nodes, units), BF16),
                pltpu.VMEM((levels + 1, wide_feat, nodes), BF16),
                pltpu.VMEM((2, slots, tall, tall), BF16),
                pltpu.VMEM((levels + 1, nodes, nodes), BF16),
                pltpu.VMEM((units, wide_feat), BF16),
                pltpu.VMEM((units, nodes), F32),
                pltpu.VMEM((wide_feat, nodes), F32),
                pltpu.VMEM((half, nodes), F32),
                pltpu.VMEM((len(wide), chunk + 8, units), F32),
                pltpu.VMEM((len(wide), chunk + 8, units), F32),
                pltpu.VMEM((len(deep), chunk, units), MID),
                pltpu.VMEM((len(wide), chunk, units), F32),
                pltpu.VMEM((len(deep), 1, units), F32),
                pltpu.VMEM((levels, half, nodes), BF16),
                pltpu.VMEM((levels, half, nodes), BF16),
                pltpu.VMEM((half, nodes), F32),
                dma((7,)),
                dma((PARTS,)),
                dma((levels,)),
                dma((levels,)),
                dma((levels + 1,)),
                dma((levels + 1,)),
                dma((1,)),
                dma((1,)),
                dma((levels,)),
                dma((levels,)),
                dma((len(wide),)),
                dma((len(wide),)),
                dma((len(deep),)),
                dma((len(deep),)),
                dma((len(wide),)),
                dma((len(wide),)),
                dma((len(deep),)),
                dma((len(deep),)),
            ],
            compiler_params=pltpu.CompilerParams(
                collective_id=0, has_side_effects=True, vmem_limit_bytes=40 * 1024 * 1024
            ),
            name="graph_layer",
        )(
            *[
                x if x is tile_count else pltpu.with_memory_space_constraint(x, pltpu.HBM)
                for x in inputs
            ]
        )
        hidden, grad_weight, grad_bias, grad_features = pl.pallas_call(
            write_kernel,
            out_shape=tuple(pltpu.HBM(shape, kind) for shape, kind in shapes),
            in_specs=[pl.BlockSpec(memory_space=pltpu.VMEM)] * len(shapes),
            out_specs=(pl.BlockSpec(memory_space=pltpu.HBM),) * len(shapes),
            scratch_shapes=[dma((len(shapes),))],
            name="write_results",
        )(*[pltpu.with_memory_space_constraint(x, pltpu.VMEM) for x in results])
        return hidden, grad_weight, grad_bias.reshape(units), grad_features.T

    return jax.shard_map(
        local,
        mesh=mesh,
        in_specs=(
            P("rows", "cols"),
            P("rows", None, None),
            P("rows"),
            P("rows"),
            P("rows"),
            P("rows"),
            P(None, "cols"),
            P("cols"),
            P("rows", "cols"),
        ),
        out_specs=(P("rows", "cols"), P(None, "cols"), P("cols"), P("rows", "cols")),
        check_vma=False,
    )
```
